512 devices in a mesh: seq: 64 (over y, x, core), chan: 8 (over z).
Axes of the slice: x: 4, y: 8, z: 8, core: 2. Of those that a mesh axis runs over, the one named last changes fastest.
Arguments:
- streams: bfloat16 [3, 16384, 8192], P(None, 'seq', 'chan'), may hold values from -6 to 6
- short_filter: float32 [3, 3, 8192], P(None, None, 'chan'), may hold values from -3 to 3
- pole_rates: float32 [16, 8192], P(None, 'chan'), may hold values from 6.1035157e-06 to 0.03
- residues: float32 [16, 8192], P(None, 'chan'), may hold values from -3 to 3
- direct: float32 [8192], P('chan'), may hold values from -3 to 3
- doc_lengths: int32 [4], replicated, may hold values from 1 to 8192, 16384 in all
- targets: int32 [16384], P('seq'), may hold values from 0 to 511
- unembed: bfloat16 [8192, 512], P('chan'), may hold values from -0.7 to 0.7
Outputs:
- gated_out: bfloat16 [16384, 8192], P('seq', 'chan')
- token_loss: float32 [16384], P('seq')
The draws below stay inside these ranges and needn't reach their ends.
All inputs are finite; a program needn't handle non-finite values.
Results may differ from the reference program's by a relative error of at most 0.012.
Values may be sent and summed in bfloat16 or wider, within the bound.
No kernel may reach another device: no remote copies, remote signals or barrier semaphores. Data moves between devices by JAX's collectives and lax.ppermute only.
A program may use at most 64 MiB of HBM per device.

```python
import math
import jax
import jax.numpy as jnp
import numpy as np
from jax import lax

D = 8192
POLES = 16
VOCAB = 512
TAPS = 3
DOCS = 4
TOKENS = 16384


def draw_unembed(key, part):
    key = jax.random.fold_in(key, 7)
    key_vals = jax.random.fold_in(key, 0)
    col_scale = 8.0
    base_vals = jnp.clip(jax.random.normal(key_vals, (D, VOCAB), jnp.float32), -4.0, 4.0)
    scaled = jnp.clip(base_vals * col_scale * (1.5 / math.sqrt(D)), -0.7, 0.7)
    return scaled.astype(jnp.bfloat16)


def with_ends(drawn, rng, least, high):
    extent = drawn.shape
    spot = [jax.random.randint(jax.random.fold_in(rng, axis), (), 0, extent[axis]) for axis in range(len(extent))]
    drawn = drawn.at[tuple(spot)].set(least)
    longest = extent.index(max(extent))
    spot[longest] = (spot[longest] + 1) % extent[longest]
    return drawn.at[tuple(spot)].set(high)


def block_scale(key, shape, pieces, low, high):
    gain = 1.0
    for dim, parts in pieces:
        steps = jax.random.uniform(jax.random.fold_in(jax.random.fold_in(key, 6), dim), (parts,), jnp.float32, low / len(pieces), high / len(pieces))
        gain = gain * jnp.repeat(jnp.exp(steps), shape[dim] // parts).reshape((-1,) + (1,) * (len(shape) - 1 - dim))
    return gain


def cumulative_ranks(number_of, lean):
    weights = [(1 << 20) // math.isqrt(standing ** lean) + 1 for standing in range(1, number_of + 1)]
    spread = 1 + sum(weights) // (1 << 30)
    return np.cumsum(np.array([max(1, weight // spread) for weight in weights]))


def skewed_ids(stream_key, shape, count, lean):
    grid = cumulative_ranks(count, lean)
    ticket = jax.random.randint(jax.random.fold_in(stream_key, 1), shape, 0, int(grid[count - 1]))
    grade = jnp.searchsorted(jnp.asarray(grid, jnp.int32), ticket, side="right")
    return jax.random.permutation(jax.random.fold_in(stream_key, 2), count)[grade].astype(jnp.int32)


def split_up(amount, total, reach, skew):
    portions = [(1 << 20) // math.isqrt(grade ** skew) + 1 for grade in range(2, amount + 1)]
    surplus, given = total - reach - (amount - 1), [1] * (amount - 1)
    while surplus > 0:
        candidates = [i for i in range(amount - 1) if given[i] < reach]
        pool, left = sum([portions[i] for i in candidates]), surplus
        for i in candidates:
            more = min(reach - given[i], max(1, left * portions[i] // pool), surplus)
            given[i] = given[i] + more
            surplus = surplus - more
    return np.array([reach] + given)


def uneven(key, number_of, total, most, slope):
    if number_of == 2:
        one = jax.random.randint(key, (), max(1, total - most), min(most, total - 1) + 1)
        return jnp.stack([one, total - one])
    sizes = jnp.asarray(split_up(number_of, total, most, slope), jnp.int32)
    twos = (number_of - 1) // 2
    giver, taker = sizes[1:1 + 2 * twos:2], sizes[2:2 + 2 * twos:2]
    slack = jnp.minimum(giver - 1, most - taker)
    passed = jax.random.randint(jax.random.fold_in(key, 1), (twos,), 0, 1 << 20) % (slack + 1)
    sizes = sizes.at[1:1 + 2 * twos:2].set(giver - passed).at[2:2 + 2 * twos:2].set(taker + passed)
    return sizes[jax.random.permutation(jax.random.fold_in(key, 2), number_of)]


def bell_draw(own_key, extent, scale, bound, cuts=(), held_as=jnp.bfloat16):
    factor_of = block_scale(own_key, extent, cuts, -0.22, 0.18) if cuts else 1.0
    values = jax.random.normal(own_key, extent, jnp.float32) * scale * factor_of
    return jnp.minimum(jnp.maximum(values, -bound), bound).astype(held_as)


def setup_inputs(seed: int = 0) -> dict:
    keys = jax.random.split(jax.random.key(seed), 9)
    streams = bell_draw(keys[0], (3, TOKENS, D), 1.0, 6.0, ((1, 64), (2, 8)))
    short_filter = bell_draw(keys[1], (3, TAPS, D), 0.6, 3.0, ((2, 8),), jnp.float32)
    pole_rates = jnp.clip(jnp.exp(math.log(0.03) - 8.500088 * jax.random.uniform(keys[2], (POLES, D), jnp.float32) ** block_scale(keys[2], (POLES, D), ((1, 8),), -0.2, 0.2)), 6.10351571594947e-06, 0.03)
    residues = bell_draw(keys[3], (POLES, D), 0.5, 3.0, ((1, 8),), jnp.float32)
    direct = bell_draw(keys[4], (D,), 0.5, 3.0, ((0, 8),), jnp.float32)
    doc_lengths = uneven(keys[5], DOCS, TOKENS, TOKENS // 2, 0).astype(jnp.int32)
    targets = with_ends(skewed_ids(keys[6], (TOKENS,), VOCAB, 2), jax.random.fold_in(keys[6], 3), 0, VOCAB - 1).astype(jnp.int32)
    unembed = draw_unembed(jax.random.fold_in(keys[8], 71), 0)
    return {"streams": streams, "short_filter": short_filter, "pole_rates": pole_rates, "residues": residues, "direct": direct, "doc_lengths": doc_lengths, "targets": targets, "unembed": unembed}


def starts_of(doc_lengths, position):
    doc_first = jnp.cumsum(doc_lengths) - doc_lengths
    chosen = jnp.where(doc_first[None, :] <= position[:, None], doc_first[None, :], 0)
    return jnp.max(chosen, axis=1).astype(jnp.int32)


def reference(streams, short_filter, pole_rates, residues, direct, doc_lengths, targets, unembed):
    position = jnp.arange(TOKENS, dtype=jnp.int32)
    doc_start = starts_of(doc_lengths, position)
    widened = streams.astype(jnp.float32)
    filtered = short_filter[:, 0, None, :] * widened
    for shift_by in range(1, TAPS):
        moved = jnp.pad(widened, ((0, 0), (shift_by, 0), (0, 0)))[:, :TOKENS]
        in_doc = (position - shift_by >= doc_start).astype(jnp.float32)
        filtered = filtered + short_filter[:, shift_by, None, :] * moved * in_doc[None, :, None]
    driver = filtered[1] * filtered[2]
    decay = jnp.exp(-pole_rates)
    inflow = 1.0 - decay
    keep_state = (doc_start < position).astype(jnp.float32)

    def advance(state, inputs):
        drive_row, keep_row = inputs
        state = decay * keep_row * state + inflow * drive_row[None, :]
        return state, jnp.sum(residues * state, axis=0)

    _, long_out = lax.scan(advance, jnp.zeros((POLES, D), jnp.float32), (driver, keep_state))
    gated_out = (filtered[0] * (long_out + direct[None, :] * driver)).astype(jnp.bfloat16)
    logits = jnp.dot(gated_out, unembed, preferred_element_type=jnp.float32)
    peak = jnp.max(logits, axis=1)
    exp_total = jnp.sum(jnp.exp(logits - peak[:, None]), axis=1)
    vocab_ids = jnp.arange(VOCAB, dtype=jnp.int32)
    picked = jnp.sum(jnp.where(targets[:, None] == vocab_ids[None, :], logits, 0.0), axis=1)
    return gated_out, peak + jnp.log(exp_total) - picked
```

```python
import functools

import jax
import jax.numpy as jnp
from jax import lax
from jax.experimental import pallas as pl
from jax.experimental.pallas import tpu as pltpu
from jax.sharding import PartitionSpec as P

F32 = jnp.float32
BF16 = jnp.bfloat16
LANES = 128
SUBS = 8
VMEM_LIMIT = 48 * 1024 * 1024


def start_positions(docs_ref, count):
    starts = [jnp.int32(0)]
    for i in range(count - 1):
        starts.append(starts[-1] + docs_ref[i])
    return starts


def no_start_in(starts, low, high):
    clean = jnp.float32(1.0)
    for s in starts:
        clean = jnp.where((s >= low) & (s < high), jnp.float32(0.0), clean)
    return clean


def keep_rows(starts, position):
    keep = jnp.ones(position.shape, F32)
    for s in starts:
        keep = jnp.where(position == s, 0.0, keep)
    return keep


def shifted_down(rows, top):
    sub = lax.broadcasted_iota(jnp.int32, rows.shape, 0)
    return jnp.where(sub == 0, top, pltpu.roll(rows, 1, 0))


def filter_steps(load, halo, taps, keep_at, keep_before, steps):
    last = load(steps - 1)
    previous = shifted_down(last, halo[1:2])
    masked_before = keep_before * shifted_down(load(steps - 2), halo[0:1])
    for j in range(steps):
        now = load(j)
        keep = keep_at(j)
        masked = keep * previous
        yield taps[0] * now + taps[1] * masked + taps[2] * (keep * masked_before)
        masked_before = masked
        previous = now


def first_kernel(
    docs_ref, first_ref, streams_ref, halo_ref, taps_ref, rates_ref,
    ends_ref, chunk_ref, driver_ref, query_ref,
    keep_scr, tail_scr, wide_scr, end_scr,
):
    poles, chans = rates_ref.shape
    block_len = streams_ref.shape[1]
    steps = block_len // SUBS
    first = first_ref[0]
    starts = start_positions(docs_ref, docs_ref.shape[0])
    base = first + steps * lax.broadcasted_iota(jnp.int32, (SUBS, LANES), 0)
    keep_before = keep_rows(starts, base - 1)
    tail = jnp.ones((SUBS, LANES), F32)
    for j in reversed(range(steps)):
        keep = keep_rows(starts, base + j)
        keep_scr[j * SUBS : (j + 1) * SUBS] = keep
        tail_scr[j * SUBS : (j + 1) * SUBS] = tail
        tail = tail * keep
    sub = lax.broadcasted_iota(jnp.int32, (SUBS, LANES), 0)
    reach = [tail]
    for k in (1, 2):
        reach.append(reach[-1] * jnp.where(sub >= k, pltpu.roll(reach[-1], k, 0), 0.0))
    reach = [jnp.where(sub >= k, r, 0.0) for k, r in zip((1, 2, 4), reach)]

    def group(g, carry):
        lanes = pl.ds(pl.multiple_of(g * LANES, LANES), LANES)
        for i in range(3):
            wide_scr[i] = streams_ref[i, :, lanes].astype(F32)

        def steps_of(i):
            halo = halo_ref[i, :, lanes].astype(F32)
            taps = [
                jnp.broadcast_to(taps_ref[i, n : n + 1, lanes], (SUBS, LANES)) for n in range(3)
            ]
            return filter_steps(
                lambda j: wide_scr[i, pl.ds(j, SUBS, stride=steps), :],
                halo,
                taps,
                lambda j: keep_scr[j * SUBS : (j + 1) * SUBS],
                keep_before,
                steps,
            )

        rate = [rates_ref[p : p + 1, lanes] for p in range(poles)]
        decay = [jnp.broadcast_to(jnp.exp(-r), (SUBS, LANES)) for r in rate]
        state = [jnp.zeros((SUBS, LANES), F32) for _ in range(poles)]
        for j, (key, value) in enumerate(zip(steps_of(1), steps_of(2))):
            rows = slice(j * SUBS, (j + 1) * SUBS)
            driver = key * value
            driver_ref[rows, lanes] = driver
            masked = driver * tail_scr[rows]
            state = [d * s + masked for d, s in zip(decay, state)]
        for j, query in enumerate(steps_of(0)):
            query_ref[j * SUBS : (j + 1) * SUBS, lanes] = query
        for p in range(poles):
            power = jnp.broadcast_to(jnp.exp(-steps * rate[p]), (SUBS, LANES))
            total = state[p]
            for k, r in zip((1, 2, 4), reach):
                total = total + (power * r) * pltpu.roll(total, k, 0)
                power = power * power
            chunk_ref[p, :, lanes] = total
            end_scr[p : p + 1, lanes] = total[SUBS - 1 : SUBS]
        return carry

    lax.fori_loop(0, chans // LANES, group, 0)
    ends = end_scr[...].astype(BF16)
    for i in range(ends_ref.shape[0]):
        ends_ref[i] = ends


def row_kernel(docs_ref, first_ref, rates_ref, ends_ref, totals_ref, before_ref, *, block_len):
    members = ends_ref.shape[0]
    first = first_ref[0]
    me = lax.rem(lax.div(first, block_len), members)
    row_first = first - me * block_len
    starts = start_positions(docs_ref, docs_ref.shape[0])
    transfer = jnp.exp(-rates_ref[...] * block_len)
    total = jnp.zeros(transfer.shape, F32)
    before = jnp.zeros(transfer.shape, F32)
    for j in range(members):
        before = jnp.where(me == j, total, before)
        low = row_first + j * block_len
        total = (transfer * no_start_in(starts, low, low + block_len)) * total + ends_ref[j].astype(F32)
    before_ref[...] = before
    rounded = total.astype(BF16)
    for i in range(totals_ref.shape[0]):
        totals_ref[i] = rounded


def out_kernel(
    docs_ref, first_ref, rates_ref, residues_ref, direct_ref, totals_ref, before_ref,
    chunk_ref, driver_ref, query_ref, unembed_ref,
    gated_ref, logits_ref,
    keep_scr, clean_scr, arriving_scr, out_scr,
    *, block_len, row_members,
):
    poles, chans = rates_ref.shape
    steps = block_len // SUBS
    first = first_ref[0]
    block = lax.div(first, block_len)
    row = lax.div(block, row_members)
    me = lax.rem(block, row_members)
    row_len = block_len * row_members
    starts = start_positions(docs_ref, docs_ref.shape[0])

    rates = rates_ref[...]
    row_transfer = jnp.exp(-rates * row_len)
    total = jnp.zeros(rates.shape, F32)
    for j in range(totals_ref.shape[0]):
        low = j * row_len
        clean = no_start_in(starts, low, low + row_len)
        moved = (row_transfer * clean) * total + totals_ref[j].astype(F32)
        total = jnp.where(j < row, moved, total)
    within = jnp.exp(-rates * (me * block_len).astype(F32)) * no_start_in(starts, row * row_len, first)
    arriving_scr[...] = before_ref[...] + within * total

    sub = lax.broadcasted_iota(jnp.int32, (SUBS, LANES), 0)
    base = first + steps * sub
    clean = jnp.ones((SUBS, LANES), F32)
    for j in range(steps):
        keep = keep_rows(starts, base + j)
        keep_scr[j * SUBS : (j + 1) * SUBS] = keep
    for s in starts:
        clean = jnp.where((s >= first) & (s < base), 0.0, clean)
    clean_scr[...] = clean

    def group(g, carry):
        lanes = pl.ds(pl.multiple_of(g * LANES, LANES), LANES)
        decay, weight, state = [], [], []
        for p in range(poles):
            rate = jnp.broadcast_to(rates_ref[p : p + 1, lanes], (SUBS, LANES))
            once = jnp.exp(-rate)
            decay.append(once)
            weight.append(residues_ref[p : p + 1, lanes] * (1.0 - once))
            carried = jnp.exp(-rate * (steps * sub).astype(F32)) * clean_scr[...]
            before = jnp.where(sub == 0, 0.0, pltpu.roll(chunk_ref[p, :, lanes], 1, 0))
            state.append(before + carried * arriving_scr[p : p + 1, lanes])
        direct = jnp.broadcast_to(direct_ref[0:1, lanes], (SUBS, LANES))
        for j in range(steps):
            rows = slice(j * SUBS, (j + 1) * SUBS)
            driver = driver_ref[rows, lanes]
            keep = keep_scr[rows]
            state = [d * (keep * s) + driver for d, s in zip(decay, state)]
            terms = [w * s for w, s in zip(weight, state)] + [direct * driver]
            while len(terms) > 1:
                paired = [a + b for a, b in zip(terms[::2], terms[1::2])]
                terms = paired + ([terms[-1]] if len(terms) % 2 else [])
            out_scr[pl.ds(j, SUBS, stride=steps), :] = query_ref[rows, lanes] * terms[0]
        gated_ref[:, lanes] = out_scr[...].astype(BF16)
        return carry

    lax.fori_loop(0, chans // LANES, group, 0)
    logits = jnp.dot(gated_ref[...], unembed_ref[...], preferred_element_type=F32).astype(BF16)
    share = logits_ref.shape[1]
    for i in range(logits_ref.shape[0]):
        logits_ref[i] = logits[i * share : (i + 1) * share]


def loss_kernel(place_ref, targets_ref, parts_ref, loss_ref):
    members, share, vocab = parts_ref.shape
    logits = parts_ref[0].astype(F32)
    for i in range(1, members):
        logits = logits + parts_ref[i].astype(F32)
    first = place_ref[0] * share
    row = lax.broadcasted_iota(jnp.int32, (share, 1), 0)
    target = jnp.zeros((share, 1), jnp.int32)
    for t in range(share):
        target = jnp.where(row == t, targets_ref[first + t], target)
    peak = jnp.max(logits, axis=1, keepdims=True)
    total = jnp.sum(jnp.exp(logits - peak), axis=1, keepdims=True)
    ids = lax.broadcasted_iota(jnp.int32, logits.shape, 1)
    picked = jnp.sum(jnp.where(ids == target, logits, 0.0), axis=1, keepdims=True)
    loss = peak + jnp.log(total) - picked
    spread = lax.broadcasted_iota(jnp.int32, (share, share), 0) == lax.broadcasted_iota(
        jnp.int32, (share, share), 1
    )
    line = jnp.sum(jnp.where(spread, loss, 0.0), axis=0, keepdims=True)
    for i in range(loss_ref.shape[0]):
        loss_ref[i] = line


def in_vmem(count):
    return [pl.BlockSpec(memory_space=pltpu.VMEM)] * count


def in_smem(count):
    return [pl.BlockSpec(memory_space=pltpu.SMEM)] * count


PARAMS = pltpu.CompilerParams(vmem_limit_bytes=VMEM_LIMIT)


def local(row_members, streams, short_filter, pole_rates, residues, direct, doc_lengths, targets, unembed):
    block_len, chans = streams.shape[1:]
    poles = pole_rates.shape[0]
    vocab = unembed.shape[1]
    seq, chan = lax.axis_size("seq"), lax.axis_size("chan")
    rows = seq // row_members
    share = block_len // chan
    steps = block_len // SUBS
    block = lax.axis_index("seq")
    first = (block * block_len).astype(jnp.int32).reshape(1)
    place = lax.axis_index("chan").astype(jnp.int32).reshape(1)
    halo = lax.ppermute(
        streams[:, block_len - 2 :, :], "seq", [(i, i + 1) for i in range(seq - 1)]
    )
    ends, chunks, driver, query = pl.pallas_call(
        first_kernel,
        out_shape=(
            jax.ShapeDtypeStruct((row_members, poles, chans), BF16),
            jax.ShapeDtypeStruct((poles, SUBS, chans), F32),
            jax.ShapeDtypeStruct((block_len, chans), F32),
            jax.ShapeDtypeStruct((block_len, chans), F32),
        ),
        in_specs=in_smem(2) + in_vmem(4),
        out_specs=in_vmem(4),
        scratch_shapes=[
            pltpu.VMEM((block_len, LANES), F32),
            pltpu.VMEM((block_len, LANES), F32),
            pltpu.VMEM((3, block_len, LANES), F32),
            pltpu.VMEM((poles, chans), F32),
        ],
        compiler_params=PARAMS,
        name="block_states",
    )(doc_lengths, first, streams, halo, short_filter, pole_rates)
    along_row = [[r * row_members + i for i in range(row_members)] for r in range(rows)]
    across_rows = [[r * row_members + i for r in range(rows)] for i in range(row_members)]
    ends = lax.all_to_all(ends, "seq", 0, 0, axis_index_groups=along_row)
    totals, before = pl.pallas_call(
        functools.partial(row_kernel, block_len=block_len),
        out_shape=(
            jax.ShapeDtypeStruct((rows, poles, chans), BF16),
            jax.ShapeDtypeStruct((poles, chans), F32),
        ),
        in_specs=in_smem(2) + in_vmem(2),
        out_specs=in_vmem(2),
        compiler_params=PARAMS,
        name="row_states",
    )(doc_lengths, first, pole_rates, ends)
    totals = lax.all_to_all(totals, "seq", 0, 0, axis_index_groups=across_rows)
    gated, logits = pl.pallas_call(
        functools.partial(out_kernel, block_len=block_len, row_members=row_members),
        out_shape=(
            jax.ShapeDtypeStruct((block_len, chans), BF16),
            jax.ShapeDtypeStruct((chan, share, vocab), BF16),
        ),
        in_specs=in_smem(2) + in_vmem(9),
        out_specs=in_vmem(2),
        scratch_shapes=[
            pltpu.VMEM((block_len, LANES), F32),
            pltpu.VMEM((SUBS, LANES), F32),
            pltpu.VMEM((poles, chans), F32),
            pltpu.VMEM((block_len, LANES), F32),
        ],
        compiler_params=PARAMS,
        name="gated_logits",
    )(
        doc_lengths, first, pole_rates, residues, direct[None], totals, before,
        chunks, driver, query, unembed,
    )
    parts = lax.all_to_all(logits, "chan", 0, 0)
    losses = pl.pallas_call(
        loss_kernel,
        out_shape=jax.ShapeDtypeStruct((chan, 1, share), F32),
        in_specs=in_smem(2) + in_vmem(1),
        out_specs=pl.BlockSpec(memory_space=pltpu.VMEM),
        compiler_params=PARAMS,
        name="token_losses",
    )(place, targets, parts)
    losses = lax.all_to_all(losses, "chan", 0, 0)
    return gated, losses.reshape(block_len)


def solution(mesh):
    seq = mesh.shape["seq"]
    row_members = 8 if seq % 8 == 0 else seq
    in_specs = (
        P(None, "seq", "chan"),
        P(None, None, "chan"),
        P(None, "chan"),
        P(None, "chan"),
        P("chan"),
        P(),
        P("seq"),
        P("chan", None),
    )
    out_specs = (P("seq", "chan"), P("seq"))
    return jax.shard_map(
        functools.partial(local, row_members),
        mesh=mesh,
        in_specs=in_specs,
        out_specs=out_specs,
        check_vma=False,
    )
```

```python
import functools

import jax
import jax.numpy as jnp
from jax import lax
from jax.experimental import pallas as pl
from jax.experimental.pallas import tpu as pltpu
from jax.sharding import PartitionSpec as P

F32 = jnp.float32
BF16 = jnp.bfloat16
LANES = 128
SUBS = 8
PITCH = 40
VMEM_LIMIT = 16 * 1024 * 1024


def start_positions(docs_ref, count):
    starts = [jnp.int32(0)]
    for i in range(count - 1):
        starts.append(starts[-1] + docs_ref[i])
    return starts


def no_start_in(starts, low, high):
    clean = jnp.float32(1.0)
    for s in starts:
        clean = jnp.where((s >= low) & (s < high), jnp.float32(0.0), clean)
    return clean


def keep_rows(starts, position):
    keep = jnp.ones(position.shape, F32)
    for s in starts:
        keep = jnp.where(position == s, 0.0, keep)
    return keep


def shifted_down(rows, top):
    sub = lax.broadcasted_iota(jnp.int32, rows.shape, 0)
    return jnp.where(sub == 0, top, pltpu.roll(rows, 1, 0))


def filter_steps(load, halo, taps, keep_at, keep_before, steps):
    last = load(steps - 1)
    previous = shifted_down(last, halo[1:2])
    masked_before = keep_before * shifted_down(load(steps - 2), halo[0:1])
    for j in range(steps):
        now = load(j)
        keep = keep_at(j)
        masked = keep * previous
        yield taps[0] * now + taps[1] * masked + taps[2] * (keep * masked_before)
        masked_before = masked
        previous = now


def first_kernel(
    docs_hbm, streams_hbm, taps_hbm, rates_hbm,
    work_ref,
    docs_ref, streams_ref, taps_ref, rates_ref, keep_scr, tail_scr, wide_scr, sems, group_sems,
):
    poles, chans = rates_ref.shape
    block_len = streams_ref.shape[1]
    steps = block_len // SUBS
    groups = chans // LANES
    copies = [
        pltpu.make_async_copy(docs_hbm, docs_ref, sems.at[0]),
        pltpu.make_async_copy(taps_hbm, taps_ref, sems.at[1]),
        pltpu.make_async_copy(rates_hbm, rates_ref, sems.at[2]),
    ]

    def group_copy(g):
        lanes = pl.ds(pl.multiple_of(g * LANES, LANES), LANES)
        return pltpu.make_async_copy(
            streams_hbm.at[1:3, :, lanes], streams_ref.at[:, :, lanes], group_sems.at[g]
        )

    for c in copies:
        c.start()
    for g in range(groups):
        group_copy(g).start()
    first = lax.axis_index("seq") * block_len
    for c in copies:
        c.wait()
    starts = start_positions(docs_ref, docs_ref.shape[0])
    base = first + steps * lax.broadcasted_iota(jnp.int32, (SUBS, LANES), 0)
    keep_before = keep_rows(starts, base - 1)
    tail = jnp.ones((SUBS, LANES), F32)
    for j in reversed(range(steps)):
        keep = keep_rows(starts, base + j)
        keep_scr[j * SUBS : (j + 1) * SUBS] = keep
        tail_scr[j * SUBS : (j + 1) * SUBS] = tail
        tail = tail * keep
    nothing = jnp.zeros((2, LANES), F32)

    def group(g, carry):
        group_copy(g).wait()
        lanes = pl.ds(pl.multiple_of(g * LANES, LANES), LANES)
        for i in range(2):
            for s in range(SUBS):
                wide_scr[i, s * PITCH : s * PITCH + steps] = streams_ref[
                    i, s * steps : (s + 1) * steps, lanes
                ].astype(F32)

        def steps_of(i):
            taps = [
                jnp.broadcast_to(taps_ref[i + 1, n : n + 1, lanes], (SUBS, LANES))
                for n in range(3)
            ]
            return filter_steps(
                lambda j: wide_scr[i, pl.ds(j, SUBS, stride=PITCH), :],
                nothing,
                taps,
                lambda j: keep_scr[j * SUBS : (j + 1) * SUBS],
                keep_before,
                steps,
            )

        decay = [
            jnp.broadcast_to(jnp.exp(-rates_ref[p : p + 1, lanes]), (SUBS, LANES))
            for p in range(poles)
        ]
        state = [jnp.zeros((SUBS, LANES), F32) for _ in range(poles)]
        for j, (key, value) in enumerate(zip(steps_of(0), steps_of(1))):
            rows = slice(j * SUBS, (j + 1) * SUBS)
            if j < 2:
                work_ref[block_len + j : block_len + 1 + j, lanes] = key[0:1]
                work_ref[block_len + 2 + j : block_len + 3 + j, lanes] = value[0:1]
            driver = key * value
            work_ref[rows, lanes] = driver
            masked = driver * tail_scr[rows]
            state = [d * s + masked for d, s in zip(decay, state)]
        for p in range(poles):
            at = block_len + SUBS * (1 + p)
            work_ref[at : at + SUBS, lanes] = state[p]
        return carry

    lax.fori_loop(0, groups, group, 0)


def corrected(starts, first, steps, halo_ref, taps_ref, edge):
    older = no_start_in(starts, first - 1, first)
    keep = [no_start_in(starts, first + j, first + j + 1) for j in range(2)]

    def added(i):
        halo = halo_ref[i].astype(F32)
        taps = taps_ref[i]
        near = (keep[0] * taps[1:2]) * halo[1:2] + (keep[0] * older * taps[2:3]) * halo[0:1]
        return near, (keep[1] * keep[0] * taps[2:3]) * halo[1:2]

    key, value = added(1), added(2)
    drivers, changes = [], []
    for j in range(2):
        old_key, old_value = edge[j : j + 1], edge[2 + j : 3 + j]
        driver = (old_key + key[j]) * (old_value + value[j])
        counts = no_start_in(starts, first + j + 1, first + steps)
        drivers.append(driver)
        changes.append(counts * (driver - old_key * old_value))
    return drivers, changes


def chunk_reach(starts, first, steps):
    sub = lax.broadcasted_iota(jnp.int32, (SUBS, LANES), 0)
    base = first + steps * sub
    clean = jnp.ones((SUBS, LANES), F32)
    for s in starts:
        clean = jnp.where((s >= base) & (s < base + steps), 0.0, clean)
    reach = [clean]
    for k in (1, 2):
        reach.append(reach[-1] * jnp.where(sub >= k, pltpu.roll(reach[-1], k, 0), 0.0))
    return [jnp.where(sub >= k, r, 0.0) for k, r in zip((1, 2, 4), reach)]


def chunk_ends(state, young, power, reach):
    sub = lax.broadcasted_iota(jnp.int32, (SUBS, LANES), 0)
    total = state + jnp.where(sub == 0, young, 0.0)
    power = jnp.broadcast_to(power, (SUBS, LANES))
    for k, r in zip((1, 2, 4), reach):
        total = total + (power * r) * pltpu.roll(total, k, 0)
        power = power * power
    return total


def join_kernel(
    docs_ref, halo_ref, taps_ref, rates_ref, residues_ref, work_ref,
    ends_ref, old_scr, young_scr, end_scr,
    *, block_len,
):
    poles, chans = rates_ref.shape
    steps = block_len // SUBS
    first = lax.axis_index("seq") * block_len
    starts = start_positions(docs_ref, docs_ref.shape[0])
    edge = work_ref[block_len : block_len + SUBS]
    _, changes = corrected(starts, first, steps, halo_ref, taps_ref, edge)
    rates = rates_ref[...]
    young_scr[...] = jnp.exp(-rates * (steps - 1)) * changes[0] + jnp.exp(-rates * (steps - 2)) * changes[1]
    old_scr[...] = jnp.exp(-rates * steps)
    reach = chunk_reach(starts, first, steps)
    for g in range(chans // LANES):
        lanes = slice(g * LANES, (g + 1) * LANES)
        for p in range(poles):
            at = block_len + SUBS * (1 + p)
            total = chunk_ends(
                work_ref[at : at + SUBS, lanes],
                young_scr[p : p + 1, lanes],
                old_scr[p : p + 1, lanes],
                reach,
            )
            end_scr[p : p + 1, lanes] = total[SUBS - 1 : SUBS]
    decays = jnp.exp(-rates)
    ends = (residues_ref[...] * ((1.0 - decays) * decays) * end_scr[...]).astype(BF16)
    for i in range(ends_ref.shape[0]):
        ends_ref[i] = ends


def row_kernel(docs_ref, rates_ref, ends_ref, totals_ref, *, block_len):
    members = ends_ref.shape[0]
    block = lax.axis_index("seq")
    first = block * block_len
    me = lax.rem(block, members)
    row_first = first - me * block_len
    starts = start_positions(docs_ref, docs_ref.shape[0])
    transfer = jnp.exp(-rates_ref[...] * block_len)
    total = jnp.zeros(transfer.shape, F32)
    before = jnp.zeros(transfer.shape, F32)
    for j in range(members):
        before = jnp.where(me == j, total, before)
        low = row_first + j * block_len
        total = (transfer * no_start_in(starts, low, low + block_len)) * total + ends_ref[j].astype(F32)
    row = lax.div(block, members)
    for i in range(totals_ref.shape[0]):
        totals_ref[i] = jnp.where(row == i, before, total).astype(BF16)


def local_kernel(
    docs_ref, halo_ref, work_ref, streams_hbm, taps_hbm, rates_hbm, residues_hbm, direct_hbm,
    made_ref,
    stream_ref, taps_ref, rates_ref, residues_ref, direct_ref,
    keep_scr, alive_scr, weight_scr, old_scr, young_scr, first_scr, wide_scr, local_scr, sems,
    *, block_len,
):
    poles, chans = rates_ref.shape
    steps = block_len // SUBS
    copies = [
        pltpu.make_async_copy(source, target, sems.at[i])
        for i, (source, target) in enumerate(
            (
                (taps_hbm, taps_ref),
                (rates_hbm, rates_ref),
                (residues_hbm, residues_ref),
                (direct_hbm, direct_ref),
                (streams_hbm.at[0], stream_ref),
            )
        )
    ]
    for c in copies:
        c.start()
    first = lax.axis_index("seq") * block_len
    starts = start_positions(docs_ref, docs_ref.shape[0])
    sub = lax.broadcasted_iota(jnp.int32, (SUBS, LANES), 0)
    base = first + steps * sub
    for j in range(steps):
        rows = slice(j * SUBS, (j + 1) * SUBS)
        keep_scr[rows] = keep_rows(starts, base + j)
        alive = jnp.ones((SUBS, LANES), F32)
        for s in starts:
            alive = jnp.where((s >= first) & (base + j >= s), 0.0, alive)
        alive_scr[rows] = alive
    keep_before = keep_rows(starts, base - 1)
    reach = chunk_reach(starts, first, steps)
    for c in copies:
        c.wait()
    edge = work_ref[block_len : block_len + SUBS]
    drivers, changes = corrected(starts, first, steps, halo_ref, taps_ref, edge)
    rates = rates_ref[...]
    decays = jnp.exp(-rates)
    weight_scr[...] = residues_ref[...] * (1.0 - decays)
    young_scr[...] = jnp.exp(-rates * (steps - 1)) * changes[0] + jnp.exp(-rates * (steps - 2)) * changes[1]
    old_scr[...] = jnp.exp(-rates * steps)
    for j in range(2):
        first_scr[j : j + 1] = drivers[j]

    def group(g, carry):
        lanes = pl.ds(pl.multiple_of(g * LANES, LANES), LANES)
        for s in range(SUBS):
            wide_scr[s * PITCH : s * PITCH + steps] = stream_ref[
                s * steps : (s + 1) * steps, lanes
            ].astype(F32)
        decay, weight, state = [], [], []
        for p in range(poles):
            rate = jnp.broadcast_to(rates_ref[p : p + 1, lanes], (SUBS, LANES))
            decay.append(jnp.exp(-rate))
            weight.append(jnp.broadcast_to(weight_scr[p : p + 1, lanes], (SUBS, LANES)))
            at = block_len + SUBS * (1 + p)
            total = chunk_ends(
                work_ref[at : at + SUBS, lanes],
                young_scr[p : p + 1, lanes],
                old_scr[p : p + 1, lanes],
                reach,
            )
            state.append(jnp.where(sub == 0, 0.0, pltpu.roll(total, 1, 0)))
        direct = jnp.broadcast_to(direct_ref[0:1, lanes], (SUBS, LANES))
        for j in range(steps):
            rows = slice(j * SUBS, (j + 1) * SUBS)
            driver = work_ref[rows, lanes]
            if j < 2:
                driver = jnp.where(sub == 0, first_scr[j : j + 1, lanes], driver)
            keep = keep_scr[rows]
            state = [d * (keep * s) + driver for d, s in zip(decay, state)]
            local_scr[rows] = summed(
                [w * s for w, s in zip(weight, state)] + [direct * driver]
            )
        taps = [jnp.broadcast_to(taps_ref[0, n : n + 1, lanes], (SUBS, LANES)) for n in range(3)]
        queries = filter_steps(
            lambda j: wide_scr[pl.ds(j, SUBS, stride=PITCH), :],
            halo_ref[0, :, lanes].astype(F32),
            taps,
            lambda j: keep_scr[j * SUBS : (j + 1) * SUBS],
            keep_before,
            steps,
        )
        local, asked = [], []
        for j, query in enumerate(queries):
            rows = slice(j * SUBS, (j + 1) * SUBS)
            local.append(query * local_scr[rows])
            asked.append(query * alive_scr[rows])
            if j % 2 == 1:
                rows = slice((j - 1) * SUBS, (j + 1) * SUBS)
                made_ref[0, rows, lanes] = jnp.concatenate(local).astype(BF16)
                made_ref[1, rows, lanes] = jnp.concatenate(asked).astype(BF16)
                local, asked = [], []
        return carry

    lax.fori_loop(0, chans // LANES, group, 0)


def summed(terms):
    while len(terms) > 1:
        paired = [a + b for a, b in zip(terms[::2], terms[1::2])]
        terms = paired + ([terms[-1]] if len(terms) % 2 else [])
    return terms[0]


def out_kernel(
    docs_ref, totals_ref, rates_ref, made_ref, unembed_hbm,
    gated_hbm, logits_ref,
    unembed_ref, gated_ref, arriving_scr, out_scr, sum_scr, sem, gated_sems,
    *, block_len, row_members,
):
    poles, chans = rates_ref.shape
    steps = block_len // SUBS
    groups = chans // LANES
    copy = pltpu.make_async_copy(unembed_hbm, unembed_ref, sem)
    gated_copies = []
    copy.start()
    block = lax.axis_index("seq")
    first = block * block_len
    row = lax.div(block, row_members)
    me = lax.rem(block, row_members)
    row_len = block_len * row_members
    starts = start_positions(docs_ref, docs_ref.shape[0])

    rates = rates_ref[...]
    row_transfer = jnp.exp(-rates * row_len)
    total = jnp.zeros(rates.shape, F32)
    before = jnp.zeros(rates.shape, F32)
    for j in range(totals_ref.shape[0]):
        low = j * row_len
        clean = no_start_in(starts, low, low + row_len)
        arrived = totals_ref[j].astype(F32)
        before = jnp.where(j == row, arrived, before)
        total = jnp.where(j < row, (row_transfer * clean) * total + arrived, total)
    within = jnp.exp(-rates * (me * block_len).astype(F32)) * no_start_in(
        starts, row * row_len, first
    )
    arriving_scr[...] = before + within * total
    sub = lax.broadcasted_iota(jnp.int32, (SUBS, LANES), 0)

    share = logits_ref.shape[1]
    for g in range(groups):
        lanes = slice(g * LANES, (g + 1) * LANES)
        decay, fading = [], []
        for p in range(poles):
            rate = jnp.broadcast_to(rates_ref[p : p + 1, lanes], (SUBS, LANES))
            decay.append(jnp.exp(-rate))
            fading.append(
                jnp.exp(-rate * (steps * sub).astype(F32)) * arriving_scr[p : p + 1, lanes]
            )
        for j in range(steps):
            if j % 2 == 0:
                both_rows = slice(j * SUBS, (j + 2) * SUBS)
                local = made_ref[0, both_rows, lanes].astype(F32)
                asked = made_ref[1, both_rows, lanes].astype(F32)
            half = slice((j % 2) * SUBS, (j % 2 + 1) * SUBS)
            out_scr[pl.ds(j, SUBS, stride=PITCH), :] = (
                local[half] + asked[half] * summed(fading)
            )
            fading = [d * f for d, f in zip(decay, fading)]
        for s in range(SUBS):
            gated_ref[s * steps : (s + 1) * steps, lanes] = out_scr[
                s * PITCH : s * PITCH + steps
            ].astype(BF16)
        if g % 2 == 1:
            both = slice((g - 1) * LANES, (g + 1) * LANES)
            gated_copies.append(
                pltpu.make_async_copy(
                    gated_ref.at[:, both], gated_hbm.at[:, both], gated_sems.at[g // 2]
                )
            )
            gated_copies[-1].start()
            if g == 1:
                copy.wait()
            part = jnp.dot(gated_ref[:, both], unembed_ref[both], preferred_element_type=F32)
            if g == 1:
                sum_scr[...] = part
            elif g < groups - 1:
                sum_scr[...] += part
            else:
                logits = (sum_scr[...] + part).astype(BF16)
                for i in range(logits_ref.shape[0]):
                    logits_ref[i] = logits[i * share : (i + 1) * share]
    for c in gated_copies:
        c.wait()


def loss_kernel(targets_ref, parts_ref, loss_ref):
    members, share, vocab = parts_ref.shape
    logits = parts_ref[0].astype(F32)
    for i in range(1, members):
        logits = logits + parts_ref[i].astype(F32)
    place = lax.axis_index("chan")
    first = place * share
    row = lax.broadcasted_iota(jnp.int32, (share, 1), 0)
    target = jnp.zeros((share, 1), jnp.int32)
    for t in range(share):
        target = jnp.where(row == t, targets_ref[first + t], target)
    peak = jnp.max(logits, axis=1, keepdims=True)
    total = jnp.sum(jnp.exp(logits - peak), axis=1, keepdims=True)
    ids = lax.broadcasted_iota(jnp.int32, logits.shape, 1)
    picked = jnp.sum(jnp.where(ids == target, logits, 0.0), axis=1, keepdims=True)
    loss = peak + jnp.log(total) - picked
    lines, wide = loss_ref.shape[1:]
    lane = lax.broadcasted_iota(jnp.int32, (share, wide), 1)
    mine = lane == lax.rem(first, wide) + lax.broadcasted_iota(jnp.int32, (share, wide), 0)
    line = jnp.sum(jnp.where(mine, loss, 0.0), axis=0, keepdims=True)
    at = lax.broadcasted_iota(jnp.int32, (lines, wide), 0) == lax.div(first, wide)
    placed = jnp.where(at, line, 0.0)
    for i in range(loss_ref.shape[0]):
        loss_ref[i] = placed


def in_vmem(count):
    return [pl.BlockSpec(memory_space=pltpu.VMEM)] * count


def in_hbm(count):
    return [pl.BlockSpec(memory_space=pltpu.HBM)] * count


def kept_in_hbm(*arrays):
    return [pltpu.with_memory_space_constraint(x, pltpu.HBM) for x in arrays]


def kept_in_vmem(*arrays):
    return [pltpu.with_memory_space_constraint(x, pltpu.VMEM) for x in arrays]


def in_smem(count):
    return [pl.BlockSpec(memory_space=pltpu.SMEM)] * count


PARAMS = pltpu.CompilerParams(vmem_limit_bytes=VMEM_LIMIT)


def local(row_members, streams, short_filter, pole_rates, residues, direct, doc_lengths, targets, unembed):
    block_len, chans = streams.shape[1:]
    poles = pole_rates.shape[0]
    vocab = unembed.shape[1]
    seq, chan = lax.axis_size("seq"), lax.axis_size("chan")
    rows = seq // row_members
    share = block_len // chan
    groups = chans // LANES
    halo = lax.ppermute(
        streams[:, block_len - 2 :, :], "seq", [(i, i + 1) for i in range(seq - 1)]
    )
    work = pl.pallas_call(
        first_kernel,
        out_shape=pltpu.VMEM((block_len + SUBS * (1 + poles), chans), F32),
        in_specs=in_hbm(4),
        out_specs=in_vmem(1)[0],
        scratch_shapes=[
            pltpu.SMEM(doc_lengths.shape, jnp.int32),
            pltpu.VMEM((2, block_len, chans), BF16),
            pltpu.VMEM(short_filter.shape, F32),
            pltpu.VMEM(pole_rates.shape, F32),
            pltpu.VMEM((block_len, LANES), F32),
            pltpu.VMEM((block_len, LANES), F32),
            pltpu.VMEM((2, SUBS * PITCH, LANES), F32),
            pltpu.SemaphoreType.DMA((3,)),
            pltpu.SemaphoreType.DMA((groups,)),
        ],
        compiler_params=PARAMS,
        cost_estimate=pl.CostEstimate(
            flops=60 * block_len * chans, bytes_accessed=4 * streams.size, transcendentals=0
        ),
        name="block_states",
    )(*kept_in_hbm(doc_lengths, streams, short_filter, pole_rates))
    ends = pl.pallas_call(
        functools.partial(join_kernel, block_len=block_len),
        out_shape=pltpu.VMEM((row_members, poles, chans), BF16),
        in_specs=in_smem(1) + in_vmem(5),
        out_specs=in_vmem(1)[0],
        scratch_shapes=[pltpu.VMEM((poles, chans), F32)] * 3,
        compiler_params=PARAMS,
        name="joined_states",
    )(doc_lengths, halo, short_filter, pole_rates, residues, *kept_in_vmem(work))
    along_row = [[r * row_members + i for i in range(row_members)] for r in range(rows)]
    across_rows = [[r * row_members + i for r in range(rows)] for i in range(row_members)]
    ends = lax.all_to_all(ends, "seq", 0, 0, axis_index_groups=along_row)
    totals = pl.pallas_call(
        functools.partial(row_kernel, block_len=block_len),
        out_shape=pltpu.VMEM((rows, poles, chans), BF16),
        in_specs=in_smem(1) + in_vmem(2),
        out_specs=in_vmem(1)[0],
        compiler_params=PARAMS,
        name="row_states",
    )(doc_lengths, pole_rates, ends)
    totals, work, halo = lax.optimization_barrier((totals, work, halo))
    totals = lax.all_to_all(totals, "seq", 0, 0, axis_index_groups=across_rows)
    made = pl.pallas_call(
        functools.partial(local_kernel, block_len=block_len),
        out_shape=pltpu.VMEM((2, block_len, chans), BF16),
        in_specs=in_smem(1) + in_vmem(2) + in_hbm(5),
        out_specs=in_vmem(1)[0],
        scratch_shapes=[
            pltpu.VMEM((block_len, chans), BF16),
            pltpu.VMEM(short_filter.shape, F32),
            pltpu.VMEM(pole_rates.shape, F32),
            pltpu.VMEM(residues.shape, F32),
            pltpu.VMEM((1, chans), F32),
            pltpu.VMEM((block_len, LANES), F32),
            pltpu.VMEM((block_len, LANES), F32),
            pltpu.VMEM((poles, chans), F32),
            pltpu.VMEM((poles, chans), F32),
            pltpu.VMEM((poles, chans), F32),
            pltpu.VMEM((2, chans), F32),
            pltpu.VMEM((SUBS * PITCH, LANES), F32),
            pltpu.VMEM((block_len, LANES), F32),
            pltpu.SemaphoreType.DMA((5,)),
        ],
        compiler_params=PARAMS,
        cost_estimate=pl.CostEstimate(
            flops=100 * block_len * chans, bytes_accessed=8 * streams.size, transcendentals=0
        ),
        name="local_out",
    )(
        doc_lengths, halo, *kept_in_vmem(work),
        *kept_in_hbm(streams, short_filter, pole_rates, residues, direct[None]),
    )
    gated, logits = pl.pallas_call(
        functools.partial(out_kernel, block_len=block_len, row_members=row_members),
        out_shape=(
            jax.ShapeDtypeStruct((block_len, chans), BF16),
            pltpu.VMEM((chan, share, vocab), BF16),
        ),
        in_specs=in_smem(1) + in_vmem(3) + in_hbm(1),
        out_specs=in_hbm(1) + in_vmem(1),
        scratch_shapes=[
            pltpu.VMEM(unembed.shape, BF16),
            pltpu.VMEM((block_len, chans), BF16),
            pltpu.VMEM((poles, chans), F32),
            pltpu.VMEM((SUBS * PITCH, LANES), F32),
            pltpu.VMEM((block_len, vocab), F32),
            pltpu.SemaphoreType.DMA,
            pltpu.SemaphoreType.DMA((groups // 2,)),
        ],
        compiler_params=PARAMS,
        name="gated_logits",
    )(doc_lengths, totals, pole_rates, *kept_in_vmem(made), *kept_in_hbm(unembed))
    parts = lax.all_to_all(logits, "chan", 0, 0)
    losses = pl.pallas_call(
        loss_kernel,
        out_shape=pltpu.VMEM((chan, block_len // LANES, LANES), F32),
        in_specs=in_smem(1) + in_vmem(1),
        out_specs=pl.BlockSpec(memory_space=pltpu.VMEM),
        compiler_params=PARAMS,
        name="token_losses",
    )(targets, parts)
    losses = lax.all_to_all(losses, "chan", 0, 0)
    return gated, jnp.sum(losses, axis=0).reshape(block_len)


def solution(mesh):
    seq = mesh.shape["seq"]
    row_members = 8 if seq % 8 == 0 else seq
    in_specs = (
        P(None, "seq", "chan"),
        P(None, None, "chan"),
        P(None, "chan"),
        P(None, "chan"),
        P("chan"),
        P(),
        P("seq"),
        P("chan", None),
    )
    out_specs = (P("seq", "chan"), P("seq"))
    return jax.shard_map(
        functools.partial(local, row_members),
        mesh=mesh,
        in_specs=in_specs,
        out_specs=out_specs,
        check_vma=False,
    )
```

```python
import functools

import jax
import jax.numpy as jnp
from jax import lax
from jax.experimental import pallas as pl
from jax.experimental.pallas import tpu as pltpu
from jax.sharding import PartitionSpec as P

F32 = jnp.float32
BF16 = jnp.bfloat16
LANES = 128
SUBS = 8
PITCH = 40
VMEM_LIMIT = 16 * 1024 * 1024


def start_positions(docs_ref, count):
    starts = [jnp.int32(0)]
    for i in range(count - 1):
        starts.append(starts[-1] + docs_ref[i])
    return starts


def no_start_in(starts, low, high):
    clean = jnp.float32(1.0)
    for s in starts:
        clean = jnp.where((s >= low) & (s < high), jnp.float32(0.0), clean)
    return clean


def keep_rows(starts, position):
    keep = jnp.ones(position.shape, F32)
    for s in starts:
        keep = jnp.where(position == s, 0.0, keep)
    return keep


def shifted_down(rows, top):
    sub = lax.broadcasted_iota(jnp.int32, rows.shape, 0)
    return jnp.where(sub == 0, top, pltpu.roll(rows, 1, 0))


def filter_steps(load, halo, taps, keep_at, keep_before, steps):
    last = load(steps - 1)
    previous = shifted_down(last, halo[1:2])
    masked_before = keep_before * shifted_down(load(steps - 2), halo[0:1])
    for j in range(steps):
        now = load(j)
        keep = keep_at(j)
        masked = keep * previous
        yield taps[0] * now + taps[1] * masked + taps[2] * (keep * masked_before)
        masked_before = masked
        previous = now


def first_kernel(
    docs_hbm, streams_hbm, taps_hbm, rates_hbm,
    work_ref,
    docs_ref, streams_ref, taps_ref, rates_ref, keep_scr, tail_scr, wide_scr, sems, group_sems,
):
    poles, chans = rates_ref.shape
    block_len = streams_ref.shape[1]
    steps = block_len // SUBS
    groups = chans // LANES
    copies = [
        pltpu.make_async_copy(docs_hbm, docs_ref, sems.at[0]),
        pltpu.make_async_copy(taps_hbm, taps_ref, sems.at[1]),
        pltpu.make_async_copy(rates_hbm, rates_ref, sems.at[2]),
    ]

    def group_copy(g):
        lanes = pl.ds(pl.multiple_of(g * LANES, LANES), LANES)
        return pltpu.make_async_copy(
            streams_hbm.at[1:3, :, lanes], streams_ref.at[:, :, lanes], group_sems.at[g]
        )

    for c in copies:
        c.start()
    for g in range(groups):
        group_copy(g).start()
    first = lax.axis_index("seq") * block_len
    for c in copies:
        c.wait()
    starts = start_positions(docs_ref, docs_ref.shape[0])
    base = first + steps * lax.broadcasted_iota(jnp.int32, (SUBS, LANES), 0)
    keep_before = keep_rows(starts, base - 1)
    tail = jnp.ones((SUBS, LANES), F32)
    for j in reversed(range(steps)):
        keep = keep_rows(starts, base + j)
        keep_scr[j * SUBS : (j + 1) * SUBS] = keep
        tail_scr[j * SUBS : (j + 1) * SUBS] = tail
        tail = tail * keep
    nothing = jnp.zeros((2, LANES), F32)

    def group(g, carry):
        group_copy(g).wait()
        lanes = pl.ds(pl.multiple_of(g * LANES, LANES), LANES)
        for i in range(2):
            for s in range(SUBS):
                wide_scr[i, s * PITCH : s * PITCH + steps] = streams_ref[
                    i, s * steps : (s + 1) * steps, lanes
                ].astype(F32)

        def steps_of(i):
            taps = [
                jnp.broadcast_to(taps_ref[i + 1, n : n + 1, lanes], (SUBS, LANES))
                for n in range(3)
            ]
            return filter_steps(
                lambda j: wide_scr[i, pl.ds(j, SUBS, stride=PITCH), :],
                nothing,
                taps,
                lambda j: keep_scr[j * SUBS : (j + 1) * SUBS],
                keep_before,
                steps,
            )

        decay = [
            jnp.broadcast_to(jnp.exp(-rates_ref[p : p + 1, lanes]), (SUBS, LANES))
            for p in range(poles)
        ]
        state = [jnp.zeros((SUBS, LANES), F32) for _ in range(poles)]
        for j, (key, value) in enumerate(zip(steps_of(0), steps_of(1))):
            rows = slice(j * SUBS, (j + 1) * SUBS)
            if j < 2:
                work_ref[g, block_len + j : block_len + 1 + j] = key[0:1]
                work_ref[g, block_len + 2 + j : block_len + 3 + j] = value[0:1]
            driver = key * value
            work_ref[g, rows] = driver
            masked = driver * tail_scr[rows]
            state = [d * s + masked for d, s in zip(decay, state)]
        for p in range(poles):
            at = block_len + SUBS * (1 + p)
            work_ref[g, at : at + SUBS] = state[p]
        return carry

    lax.fori_loop(0, groups, group, 0)


def edge_marks(starts, first, steps):
    older = no_start_in(starts, first - 1, first)
    keep = [no_start_in(starts, first + j, first + j + 1) for j in range(2)]
    counts = [no_start_in(starts, first + j + 1, first + steps) for j in range(2)]
    return older, keep, counts


def corrected(marks, halo_ref, taps_ref, edge, lanes):
    older, keep, counts = marks

    def added(i):
        halo = halo_ref[i, :, lanes].astype(F32)
        taps = taps_ref[i, :, lanes]
        near = (keep[0] * taps[1:2]) * halo[1:2] + (keep[0] * older * taps[2:3]) * halo[0:1]
        return near, (keep[1] * keep[0] * taps[2:3]) * halo[1:2]

    key, value = added(1), added(2)
    drivers, changes = [], []
    for j in range(2):
        old_key, old_value = edge[j : j + 1], edge[2 + j : 3 + j]
        driver = (old_key + key[j]) * (old_value + value[j])
        drivers.append(driver)
        changes.append(counts[j] * (driver - old_key * old_value))
    return drivers, changes


def chunk_reach(starts, first, steps):
    sub = lax.broadcasted_iota(jnp.int32, (SUBS, LANES), 0)
    base = first + steps * sub
    clean = jnp.ones((SUBS, LANES), F32)
    for s in starts:
        clean = jnp.where((s >= base) & (s < base + steps), 0.0, clean)
    reach = [clean]
    for k in (1, 2):
        reach.append(reach[-1] * jnp.where(sub >= k, pltpu.roll(reach[-1], k, 0), 0.0))
    return [jnp.where(sub >= k, r, 0.0) for k, r in zip((1, 2, 4), reach)]


def chunk_ends(state, young, power, reach):
    sub = lax.broadcasted_iota(jnp.int32, (SUBS, LANES), 0)
    total = state + jnp.where(sub == 0, young, 0.0)
    power = jnp.broadcast_to(power, (SUBS, LANES))
    for k, r in zip((1, 2, 4), reach):
        total = total + (power * r) * pltpu.roll(total, k, 0)
        power = power * power
    return total


def join_kernel(
    docs_ref, halo_ref, taps_ref, rates_ref, residues_ref, work_ref, ends_ref, *, block_len
):
    poles, chans = rates_ref.shape
    steps = block_len // SUBS
    first = lax.axis_index("seq") * block_len
    starts = start_positions(docs_ref, docs_ref.shape[0])
    marks = edge_marks(starts, first, steps)
    clean = [
        no_start_in(starts, first + s * steps, first + (s + 1) * steps) for s in range(SUBS)
    ]
    for g in range(chans // LANES):
        lanes = slice(g * LANES, (g + 1) * LANES)
        edge = work_ref[g, block_len : block_len + SUBS]
        _, changes = corrected(marks, halo_ref, taps_ref, edge, lanes)
        rates = rates_ref[:, lanes]
        decays = jnp.exp(-rates)
        transfer = jnp.exp(-rates * steps)
        total = jnp.exp(-rates * (steps - 2)) * (decays * changes[0] + changes[1])
        for s in range(SUBS):
            if s > 0:
                total = (transfer * clean[s]) * total
            total = total + work_ref[g, pl.ds(block_len + SUBS + s, poles, stride=SUBS), :]
        ends = (residues_ref[:, lanes] * ((1.0 - decays) * decays) * total).astype(BF16)
        for i in range(ends_ref.shape[0]):
            ends_ref[i, :, lanes] = ends


def row_kernel(docs_ref, rates_ref, ends_ref, totals_ref, *, block_len):
    members = ends_ref.shape[0]
    block = lax.axis_index("seq")
    first = block * block_len
    me = lax.rem(block, members)
    row_first = first - me * block_len
    starts = start_positions(docs_ref, docs_ref.shape[0])
    transfer = jnp.exp(-rates_ref[...] * block_len)
    total = jnp.zeros(transfer.shape, F32)
    before = jnp.zeros(transfer.shape, F32)
    for j in range(members):
        before = jnp.where(me == j, total, before)
        low = row_first + j * block_len
        total = (transfer * no_start_in(starts, low, low + block_len)) * total + ends_ref[j].astype(F32)
    row = lax.div(block, members)
    rounded = total.astype(BF16)
    for i in range(totals_ref.shape[0]):
        totals_ref[i] = rounded
    totals_ref[row] = before.astype(BF16)


def local_kernel(
    docs_ref, halo_ref, work_ref, streams_hbm, taps_hbm, rates_hbm, residues_hbm, direct_hbm,
    made_ref,
    stream_ref, taps_ref, rates_ref, residues_ref, direct_ref,
    keep_scr, alive_scr, weight_scr, old_scr, young_scr, first_scr, wide_scr, local_scr, sems,
    *, block_len,
):
    poles, chans = rates_ref.shape
    steps = block_len // SUBS
    copies = [
        pltpu.make_async_copy(source, target, sems.at[i])
        for i, (source, target) in enumerate(
            (
                (taps_hbm, taps_ref),
                (rates_hbm, rates_ref),
                (residues_hbm, residues_ref),
                (direct_hbm, direct_ref),
                (streams_hbm.at[0], stream_ref),
            )
        )
    ]
    for c in copies:
        c.start()
    first = lax.axis_index("seq") * block_len
    starts = start_positions(docs_ref, docs_ref.shape[0])
    sub = lax.broadcasted_iota(jnp.int32, (SUBS, LANES), 0)
    base = first + steps * sub
    for j in range(steps):
        rows = slice(j * SUBS, (j + 1) * SUBS)
        keep_scr[rows] = keep_rows(starts, base + j)
        alive = jnp.ones((SUBS, LANES), F32)
        for s in starts:
            alive = jnp.where((s >= first) & (base + j >= s), 0.0, alive)
        alive_scr[rows] = alive
    keep_before = keep_rows(starts, base - 1)
    reach = chunk_reach(starts, first, steps)
    for c in copies:
        c.wait()
    rates = rates_ref[...]
    decays = jnp.exp(-rates)
    weight_scr[...] = residues_ref[...] * (1.0 - decays)
    older = jnp.exp(-rates * (steps - 2))
    old_scr[...] = jnp.exp(-rates * steps)
    marks = edge_marks(starts, first, steps)
    for g in range(chans // LANES):
        lanes = slice(g * LANES, (g + 1) * LANES)
        edge = work_ref[g, block_len : block_len + SUBS]
        drivers, changes = corrected(marks, halo_ref, taps_ref, edge, lanes)
        young_scr[:, lanes] = older[:, lanes] * (decays[:, lanes] * changes[0] + changes[1])
        for j in range(2):
            first_scr[j : j + 1, lanes] = drivers[j]

    def group(g, carry):
        lanes = pl.ds(pl.multiple_of(g * LANES, LANES), LANES)
        for s in range(SUBS):
            wide_scr[s * PITCH : s * PITCH + steps] = stream_ref[
                s * steps : (s + 1) * steps, lanes
            ].astype(F32)
        decay, weight, state = [], [], []
        for p in range(poles):
            rate = jnp.broadcast_to(rates_ref[p : p + 1, lanes], (SUBS, LANES))
            decay.append(jnp.exp(-rate))
            weight.append(jnp.broadcast_to(weight_scr[p : p + 1, lanes], (SUBS, LANES)))
            at = block_len + SUBS * (1 + p)
            total = chunk_ends(
                work_ref[g, at : at + SUBS],
                young_scr[p : p + 1, lanes],
                old_scr[p : p + 1, lanes],
                reach,
            )
            state.append(jnp.where(sub == 0, 0.0, pltpu.roll(total, 1, 0)))
        direct = jnp.broadcast_to(direct_ref[0:1, lanes], (SUBS, LANES))
        for j in range(steps):
            rows = slice(j * SUBS, (j + 1) * SUBS)
            driver = work_ref[g, rows]
            if j < 2:
                driver = jnp.where(sub == 0, first_scr[j : j + 1, lanes], driver)
            keep = keep_scr[rows]
            state = [d * (keep * s) + driver for d, s in zip(decay, state)]
            local_scr[rows] = summed(
                [w * s for w, s in zip(weight, state)] + [direct * driver]
            )
        taps = [jnp.broadcast_to(taps_ref[0, n : n + 1, lanes], (SUBS, LANES)) for n in range(3)]
        queries = filter_steps(
            lambda j: wide_scr[pl.ds(j, SUBS, stride=PITCH), :],
            halo_ref[0, :, lanes].astype(F32),
            taps,
            lambda j: keep_scr[j * SUBS : (j + 1) * SUBS],
            keep_before,
            steps,
        )
        local, asked = [], []
        for j, query in enumerate(queries):
            rows = slice(j * SUBS, (j + 1) * SUBS)
            local.append(query * local_scr[rows])
            asked.append(query * alive_scr[rows])
            if j % 2 == 1:
                rows = slice((j - 1) * SUBS, (j + 1) * SUBS)
                made_ref[0, rows, lanes] = jnp.concatenate(local).astype(BF16)
                made_ref[1, rows, lanes] = jnp.concatenate(asked).astype(BF16)
                local, asked = [], []
        return carry

    lax.fori_loop(0, chans // LANES, group, 0)


def summed(terms):
    while len(terms) > 1:
        paired = [a + b for a, b in zip(terms[::2], terms[1::2])]
        terms = paired + ([terms[-1]] if len(terms) % 2 else [])
    return terms[0]


def out_kernel(
    docs_ref, totals_ref, rates_ref, made_ref, unembed_hbm,
    gated_hbm, logits_ref,
    unembed_ref, gated_ref, arriving_scr, out_scr, sem, gated_sems,
    *, block_len, row_members,
):
    poles, chans = rates_ref.shape
    steps = block_len // SUBS
    groups = chans // LANES
    copy = pltpu.make_async_copy(unembed_hbm, unembed_ref, sem)
    gated_copies = []
    copy.start()
    block = lax.axis_index("seq")
    first = block * block_len
    row = lax.div(block, row_members)
    me = lax.rem(block, row_members)
    row_len = block_len * row_members
    starts = start_positions(docs_ref, docs_ref.shape[0])

    rates = rates_ref[...]
    row_transfer = jnp.exp(-rates * row_len)
    total = jnp.zeros(rates.shape, F32)
    before = jnp.zeros(rates.shape, F32)
    for j in range(totals_ref.shape[0]):
        low = j * row_len
        clean = no_start_in(starts, low, low + row_len)
        arrived = totals_ref[j].astype(F32)
        before = jnp.where(j == row, arrived, before)
        total = jnp.where(j < row, (row_transfer * clean) * total + arrived, total)
    within = jnp.exp(-rates * (me * block_len).astype(F32)) * no_start_in(
        starts, row * row_len, first
    )
    arriving_scr[...] = before + within * total
    sub = lax.broadcasted_iota(jnp.int32, (SUBS, LANES), 0)

    share = logits_ref.shape[1]
    for g in range(groups):
        lanes = slice(g * LANES, (g + 1) * LANES)
        decay, fading = [], []
        for p in range(poles):
            rate = jnp.broadcast_to(rates_ref[p : p + 1, lanes], (SUBS, LANES))
            decay.append(jnp.exp(-rate))
            fading.append(
                jnp.exp(-rate * (steps * sub).astype(F32)) * arriving_scr[p : p + 1, lanes]
            )
        for j in range(steps):
            if j % 2 == 0:
                both_rows = slice(j * SUBS, (j + 2) * SUBS)
                local = made_ref[0, both_rows, lanes].astype(F32)
                asked = made_ref[1, both_rows, lanes].astype(F32)
            half = slice((j % 2) * SUBS, (j % 2 + 1) * SUBS)
            out_scr[pl.ds(j, SUBS, stride=PITCH), :] = (
                local[half] + asked[half] * summed(fading)
            )
            fading = [d * f for d, f in zip(decay, fading)]
        for s in range(SUBS):
            gated_ref[s * steps : (s + 1) * steps, lanes] = out_scr[
                s * PITCH : s * PITCH + steps
            ].astype(BF16)
        if g % 2 == 1:
            both = slice((g - 1) * LANES, (g + 1) * LANES)
            gated_copies.append(
                pltpu.make_async_copy(
                    gated_ref.at[:, both], gated_hbm.at[:, both], gated_sems.at[g // 2]
                )
            )
            gated_copies[-1].start()
    copy.wait()
    logits = jnp.dot(gated_ref[...], unembed_ref[...], preferred_element_type=F32).astype(BF16)
    for i in range(logits_ref.shape[0]):
        logits_ref[i] = logits[i * share : (i + 1) * share]
    for c in gated_copies:
        c.wait()


def loss_kernel(targets_ref, parts_ref, loss_ref):
    members, share, vocab = parts_ref.shape
    logits = parts_ref[0].astype(F32)
    for i in range(1, members):
        logits = logits + parts_ref[i].astype(F32)
    place = lax.axis_index("chan")
    first = place * share
    row = lax.broadcasted_iota(jnp.int32, (share, 1), 0)
    target = jnp.zeros((share, 1), jnp.int32)
    for t in range(share):
        target = jnp.where(row == t, targets_ref[first + t], target)
    peak = jnp.max(logits, axis=1, keepdims=True)
    total = jnp.sum(jnp.exp(logits - peak), axis=1, keepdims=True)
    ids = lax.broadcasted_iota(jnp.int32, logits.shape, 1)
    picked = jnp.sum(jnp.where(ids == target, logits, 0.0), axis=1, keepdims=True)
    loss = peak + jnp.log(total) - picked
    lines, wide = loss_ref.shape[1:]
    lane = lax.broadcasted_iota(jnp.int32, (share, wide), 1)
    mine = lane == lax.rem(first, wide) + lax.broadcasted_iota(jnp.int32, (share, wide), 0)
    line = jnp.sum(jnp.where(mine, loss, 0.0), axis=0, keepdims=True)
    at = lax.broadcasted_iota(jnp.int32, (lines, wide), 0) == lax.div(first, wide)
    placed = jnp.where(at, line, 0.0)
    for i in range(loss_ref.shape[0]):
        loss_ref[i] = placed


def in_vmem(count):
    return [pl.BlockSpec(memory_space=pltpu.VMEM)] * count


def in_hbm(count):
    return [pl.BlockSpec(memory_space=pltpu.HBM)] * count


def kept_in_hbm(*arrays):
    return [pltpu.with_memory_space_constraint(x, pltpu.HBM) for x in arrays]


def kept_in_vmem(*arrays):
    return [pltpu.with_memory_space_constraint(x, pltpu.VMEM) for x in arrays]


def in_smem(count):
    return [pl.BlockSpec(memory_space=pltpu.SMEM)] * count


PARAMS = pltpu.CompilerParams(vmem_limit_bytes=VMEM_LIMIT)


def local(row_members, streams, short_filter, pole_rates, residues, direct, doc_lengths, targets, unembed):
    block_len, chans = streams.shape[1:]
    poles = pole_rates.shape[0]
    vocab = unembed.shape[1]
    seq, chan = lax.axis_size("seq"), lax.axis_size("chan")
    rows = seq // row_members
    share = block_len // chan
    groups = chans // LANES
    halo = lax.ppermute(
        streams[:, block_len - 2 :, :], "seq", [(i, i + 1) for i in range(seq - 1)]
    )
    work = pl.pallas_call(
        first_kernel,
        out_shape=pltpu.VMEM((groups, block_len + SUBS * (1 + poles), LANES), F32),
        in_specs=in_hbm(4),
        out_specs=in_vmem(1)[0],
        scratch_shapes=[
            pltpu.SMEM(doc_lengths.shape, jnp.int32),
            pltpu.VMEM((2, block_len, chans), BF16),
            pltpu.VMEM(short_filter.shape, F32),
            pltpu.VMEM(pole_rates.shape, F32),
            pltpu.VMEM((block_len, LANES), F32),
            pltpu.VMEM((block_len, LANES), F32),
            pltpu.VMEM((2, SUBS * PITCH, LANES), F32),
            pltpu.SemaphoreType.DMA((3,)),
            pltpu.SemaphoreType.DMA((groups,)),
        ],
        compiler_params=PARAMS,
        cost_estimate=pl.CostEstimate(
            flops=60 * block_len * chans, bytes_accessed=4 * streams.size, transcendentals=0
        ),
        name="block_states",
    )(*kept_in_hbm(doc_lengths, streams, short_filter, pole_rates))
    ends = pl.pallas_call(
        functools.partial(join_kernel, block_len=block_len),
        out_shape=pltpu.VMEM((row_members, poles, chans), BF16),
        in_specs=in_smem(1) + in_vmem(5),
        out_specs=in_vmem(1)[0],
        compiler_params=PARAMS,
        name="joined_states",
    )(doc_lengths, halo, short_filter, pole_rates, residues, *kept_in_vmem(work))
    along_row = [[r * row_members + i for i in range(row_members)] for r in range(rows)]
    across_rows = [[r * row_members + i for r in range(rows)] for i in range(row_members)]
    ends = lax.all_to_all(ends, "seq", 0, 0, axis_index_groups=along_row)
    totals = pl.pallas_call(
        functools.partial(row_kernel, block_len=block_len),
        out_shape=pltpu.VMEM((rows, poles, chans), BF16),
        in_specs=in_smem(1) + in_vmem(2),
        out_specs=in_vmem(1)[0],
        compiler_params=PARAMS,
        name="row_states",
    )(doc_lengths, pole_rates, ends)
    totals, work, halo = lax.optimization_barrier((totals, work, halo))
    totals = lax.all_to_all(totals, "seq", 0, 0, axis_index_groups=across_rows)
    made = pl.pallas_call(
        functools.partial(local_kernel, block_len=block_len),
        out_shape=pltpu.VMEM((2, block_len, chans), BF16),
        in_specs=in_smem(1) + in_vmem(2) + in_hbm(5),
        out_specs=in_vmem(1)[0],
        scratch_shapes=[
            pltpu.VMEM((block_len, chans), BF16),
            pltpu.VMEM(short_filter.shape, F32),
            pltpu.VMEM(pole_rates.shape, F32),
            pltpu.VMEM(residues.shape, F32),
            pltpu.VMEM((1, chans), F32),
            pltpu.VMEM((block_len, LANES), F32),
            pltpu.VMEM((block_len, LANES), F32),
            pltpu.VMEM((poles, chans), F32),
            pltpu.VMEM((poles, chans), F32),
            pltpu.VMEM((poles, chans), F32),
            pltpu.VMEM((2, chans), F32),
            pltpu.VMEM((SUBS * PITCH, LANES), F32),
            pltpu.VMEM((block_len, LANES), F32),
            pltpu.SemaphoreType.DMA((5,)),
        ],
        compiler_params=PARAMS,
        cost_estimate=pl.CostEstimate(
            flops=100 * block_len * chans, bytes_accessed=8 * streams.size, transcendentals=0
        ),
        name="local_out",
    )(
        doc_lengths, halo, *kept_in_vmem(work),
        *kept_in_hbm(streams, short_filter, pole_rates, residues, direct[None]),
    )
    gated, logits = pl.pallas_call(
        functools.partial(out_kernel, block_len=block_len, row_members=row_members),
        out_shape=(
            jax.ShapeDtypeStruct((block_len, chans), BF16),
            pltpu.VMEM((chan, share, vocab), BF16),
        ),
        in_specs=in_smem(1) + in_vmem(3) + in_hbm(1),
        out_specs=in_hbm(1) + in_vmem(1),
        scratch_shapes=[
            pltpu.VMEM(unembed.shape, BF16),
            pltpu.VMEM((block_len, chans), BF16),
            pltpu.VMEM((poles, chans), F32),
            pltpu.VMEM((SUBS * PITCH, LANES), F32),
            pltpu.SemaphoreType.DMA,
            pltpu.SemaphoreType.DMA((groups // 2,)),
        ],
        compiler_params=PARAMS,
        name="gated_logits",
    )(doc_lengths, totals, pole_rates, *kept_in_vmem(made), *kept_in_hbm(unembed))
    parts = lax.all_to_all(logits, "chan", 0, 0)
    losses = pl.pallas_call(
        loss_kernel,
        out_shape=pltpu.VMEM((chan, block_len // LANES, LANES), F32),
        in_specs=in_smem(1) + in_vmem(1),
        out_specs=pl.BlockSpec(memory_space=pltpu.VMEM),
        compiler_params=PARAMS,
        name="token_losses",
    )(targets, parts)
    losses = lax.all_to_all(losses, "chan", 0, 0)
    return gated, jnp.sum(losses, axis=0).reshape(block_len)


def solution(mesh):
    seq = mesh.shape["seq"]
    row_members = 8 if seq % 8 == 0 else seq
    in_specs = (
        P(None, "seq", "chan"),
        P(None, None, "chan"),
        P(None, "chan"),
        P(None, "chan"),
        P("chan"),
        P(),
        P("seq"),
        P("chan", None),
    )
    out_specs = (P("seq", "chan"), P("seq"))
    return jax.shard_map(
        functools.partial(local, row_members),
        mesh=mesh,
        in_specs=in_specs,
        out_specs=out_specs,
        check_vma=False,
    )
```

```python
import functools

import jax
import jax.numpy as jnp
from jax import lax
from jax.experimental import pallas as pl
from jax.experimental.pallas import tpu as pltpu
from jax.sharding import PartitionSpec as P

F32 = jnp.float32
BF16 = jnp.bfloat16
LANES = 128
SUBS = 8
PITCH = 40
LONGEST = 8192
VMEM_LIMIT = 16 * 1024 * 1024


def start_positions(docs_ref, count):
    starts = [jnp.int32(0)]
    for i in range(count - 1):
        starts.append(starts[-1] + docs_ref[i])
    return starts


def no_start_in(starts, low, high):
    clean = jnp.float32(1.0)
    for s in starts:
        clean = jnp.where((s >= low) & (s < high), jnp.float32(0.0), clean)
    return clean


def keep_rows(starts, position):
    keep = jnp.ones(position.shape, F32)
    for s in starts:
        keep = jnp.where(position == s, 0.0, keep)
    return keep


def shifted_down(rows, top):
    sub = lax.broadcasted_iota(jnp.int32, rows.shape, 0)
    return jnp.where(sub == 0, top, pltpu.roll(rows, 1, 0))


def filter_steps(load, halo, taps, keep_at, keep_before, steps):
    last = load(steps - 1)
    previous = shifted_down(last, halo[1:2])
    masked_before = keep_before * shifted_down(load(steps - 2), halo[0:1])
    for j in range(steps):
        now = load(j)
        keep = keep_at(j)
        masked = keep * previous
        yield taps[0] * now + taps[1] * masked + taps[2] * (keep * masked_before)
        masked_before = masked
        previous = now


def first_kernel(
    docs_hbm, streams_hbm, taps_hbm, rates_hbm,
    work_ref,
    docs_ref, streams_ref, taps_ref, rates_ref, keep_scr, tail_scr, wide_scr, sems, group_sems,
):
    poles, chans = rates_ref.shape
    block_len = streams_ref.shape[1]
    steps = block_len // SUBS
    groups = chans // LANES
    copies = [
        pltpu.make_async_copy(docs_hbm, docs_ref, sems.at[0]),
        pltpu.make_async_copy(taps_hbm, taps_ref, sems.at[1]),
        pltpu.make_async_copy(rates_hbm, rates_ref, sems.at[2]),
    ]

    def group_copy(g):
        lanes = pl.ds(pl.multiple_of(g * LANES, LANES), LANES)
        return pltpu.make_async_copy(
            streams_hbm.at[1:3, :, lanes], streams_ref.at[:, :, lanes], group_sems.at[g]
        )

    for c in copies:
        c.start()
    for g in range(groups):
        group_copy(g).start()
    first = lax.axis_index("seq") * block_len
    for c in copies:
        c.wait()
    starts = start_positions(docs_ref, docs_ref.shape[0])
    base = first + steps * lax.broadcasted_iota(jnp.int32, (SUBS, LANES), 0)
    keep_before = keep_rows(starts, base - 1)
    tail = jnp.ones((SUBS, LANES), F32)
    for j in reversed(range(steps)):
        keep = keep_rows(starts, base + j)
        keep_scr[j * SUBS : (j + 1) * SUBS] = keep
        tail_scr[j * SUBS : (j + 1) * SUBS] = tail
        tail = tail * keep
    nothing = jnp.zeros((2, LANES), F32)

    def group(g, carry):
        group_copy(g).wait()
        lanes = pl.ds(pl.multiple_of(g * LANES, LANES), LANES)
        for i in range(2):
            for s in range(SUBS):
                wide_scr[i, s * PITCH : s * PITCH + steps] = streams_ref[
                    i, s * steps : (s + 1) * steps, lanes
                ].astype(F32)

        def steps_of(i):
            taps = [
                jnp.broadcast_to(taps_ref[i + 1, n : n + 1, lanes], (SUBS, LANES))
                for n in range(3)
            ]
            return filter_steps(
                lambda j: wide_scr[i, pl.ds(j, SUBS, stride=PITCH), :],
                nothing,
                taps,
                lambda j: keep_scr[j * SUBS : (j + 1) * SUBS],
                keep_before,
                steps,
            )

        decay = [
            jnp.broadcast_to(jnp.exp(-rates_ref[p : p + 1, lanes]), (SUBS, LANES))
            for p in range(poles)
        ]
        state = [jnp.zeros((SUBS, LANES), F32) for _ in range(poles)]
        for j, (key, value) in enumerate(zip(steps_of(0), steps_of(1))):
            rows = slice(j * SUBS, (j + 1) * SUBS)
            if j < 2:
                work_ref[g, block_len + j : block_len + 1 + j] = key[0:1]
                work_ref[g, block_len + 2 + j : block_len + 3 + j] = value[0:1]
            driver = key * value
            work_ref[g, rows] = driver
            masked = driver * tail_scr[rows]
            state = [d * s + masked for d, s in zip(decay, state)]
        for p in range(poles):
            at = block_len + SUBS * (1 + p)
            work_ref[g, at : at + SUBS] = state[p]
        return carry

    lax.fori_loop(0, groups, group, 0)


def edge_marks(starts, first, steps):
    older = no_start_in(starts, first - 1, first)
    keep = [no_start_in(starts, first + j, first + j + 1) for j in range(2)]
    counts = [no_start_in(starts, first + j + 1, first + steps) for j in range(2)]
    return older, keep, counts


def corrected(marks, halo_ref, taps_ref, edge, lanes):
    older, keep, counts = marks

    def added(i):
        halo = halo_ref[i, :, lanes].astype(F32)
        taps = taps_ref[i, :, lanes]
        near = (keep[0] * taps[1:2]) * halo[1:2] + (keep[0] * older * taps[2:3]) * halo[0:1]
        return near, (keep[1] * keep[0] * taps[2:3]) * halo[1:2]

    key, value = added(1), added(2)
    drivers, changes = [], []
    for j in range(2):
        old_key, old_value = edge[j : j + 1], edge[2 + j : 3 + j]
        driver = (old_key + key[j]) * (old_value + value[j])
        drivers.append(driver)
        changes.append(counts[j] * (driver - old_key * old_value))
    return drivers, changes


def chunk_reach(starts, first, steps):
    sub = lax.broadcasted_iota(jnp.int32, (SUBS, LANES), 0)
    base = first + steps * sub
    clean = jnp.ones((SUBS, LANES), F32)
    for s in starts:
        clean = jnp.where((s >= base) & (s < base + steps), 0.0, clean)
    reach = [clean]
    for k in (1, 2):
        reach.append(reach[-1] * jnp.where(sub >= k, pltpu.roll(reach[-1], k, 0), 0.0))
    return [jnp.where(sub >= k, r, 0.0) for k, r in zip((1, 2, 4), reach)]


def chunk_ends(state, young, power, reach):
    sub = lax.broadcasted_iota(jnp.int32, (SUBS, LANES), 0)
    total = state + jnp.where(sub == 0, young, 0.0)
    power = jnp.broadcast_to(power, (SUBS, LANES))
    for k, r in zip((1, 2, 4), reach):
        total = total + (power * r) * pltpu.roll(total, k, 0)
        power = power * power
    return total


def join_kernel(
    docs_ref, halo_ref, taps_ref, rates_ref, residues_ref, work_ref, ends_ref, *, block_len
):
    poles, chans = rates_ref.shape
    steps = block_len // SUBS
    first = lax.axis_index("seq") * block_len
    starts = start_positions(docs_ref, docs_ref.shape[0])
    marks = edge_marks(starts, first, steps)
    clean = [
        no_start_in(starts, first + s * steps, first + (s + 1) * steps) for s in range(SUBS)
    ]
    for g in range(chans // LANES):
        lanes = slice(g * LANES, (g + 1) * LANES)
        edge = work_ref[g, block_len : block_len + SUBS]
        _, changes = corrected(marks, halo_ref, taps_ref, edge, lanes)
        rates = rates_ref[:, lanes]
        decays = jnp.exp(-rates)
        transfer = jnp.exp(-rates * steps)
        total = jnp.exp(-rates * (steps - 2)) * (decays * changes[0] + changes[1])
        for s in range(SUBS):
            if s > 0:
                total = (transfer * clean[s]) * total
            total = total + work_ref[g, pl.ds(block_len + SUBS + s, poles, stride=SUBS), :]
        ends = (residues_ref[:, lanes] * ((1.0 - decays) * decays) * total).astype(BF16)
        for i in range(ends_ref.shape[0]):
            ends_ref[i, :, lanes] = ends


def row_kernel(docs_ref, rates_ref, ends_ref, total_ref, before_ref, *, block_len):
    members = ends_ref.shape[0]
    block = lax.axis_index("seq")
    first = block * block_len
    me = lax.rem(block, members)
    row_first = first - me * block_len
    starts = start_positions(docs_ref, docs_ref.shape[0])
    transfer = jnp.exp(-rates_ref[...] * block_len)
    total = jnp.zeros(transfer.shape, F32)
    before = jnp.zeros(transfer.shape, F32)
    for j in range(members):
        before = jnp.where(me == j, total, before)
        low = row_first + j * block_len
        total = (transfer * no_start_in(starts, low, low + block_len)) * total + ends_ref[j].astype(F32)
    total_ref[...] = total.astype(BF16)
    before_ref[...] = before


def local_kernel(
    docs_ref, halo_ref, work_ref, taps_hbm, rates_hbm, residues_hbm, direct_hbm,
    local_ref,
    taps_ref, rates_ref, residues_ref, direct_ref,
    keep_scr, weight_scr, old_scr, young_scr, first_scr, sems,
    *, block_len,
):
    poles, chans = rates_ref.shape
    steps = block_len // SUBS
    copies = [
        pltpu.make_async_copy(source, target, sems.at[i])
        for i, (source, target) in enumerate(
            (
                (taps_hbm, taps_ref),
                (rates_hbm, rates_ref),
                (residues_hbm, residues_ref),
                (direct_hbm, direct_ref),
            )
        )
    ]
    for c in copies:
        c.start()
    first = lax.axis_index("seq") * block_len
    starts = start_positions(docs_ref, docs_ref.shape[0])
    sub = lax.broadcasted_iota(jnp.int32, (SUBS, LANES), 0)
    base = first + steps * sub
    for j in range(steps):
        keep_scr[j * SUBS : (j + 1) * SUBS] = keep_rows(starts, base + j)
    reach = chunk_reach(starts, first, steps)
    for c in copies:
        c.wait()
    rates = rates_ref[...]
    decays = jnp.exp(-rates)
    weight_scr[...] = residues_ref[...] * (1.0 - decays)
    older = jnp.exp(-rates * (steps - 2))
    old_scr[...] = jnp.exp(-rates * steps)
    marks = edge_marks(starts, first, steps)
    for g in range(chans // LANES):
        lanes = slice(g * LANES, (g + 1) * LANES)
        edge = work_ref[g, block_len : block_len + SUBS]
        drivers, changes = corrected(marks, halo_ref, taps_ref, edge, lanes)
        young_scr[:, lanes] = older[:, lanes] * (decays[:, lanes] * changes[0] + changes[1])
        for j in range(2):
            first_scr[j : j + 1, lanes] = drivers[j]

    def group(g, carry):
        lanes = pl.ds(pl.multiple_of(g * LANES, LANES), LANES)
        decays = jnp.exp(-rates_ref[:, lanes])
        decay, weight, state = [], [], []
        for p in range(poles):
            decay.append(jnp.broadcast_to(decays[p : p + 1], (SUBS, LANES)))
            weight.append(jnp.broadcast_to(weight_scr[p : p + 1, lanes], (SUBS, LANES)))
            at = block_len + SUBS * (1 + p)
            total = chunk_ends(
                work_ref[g, at : at + SUBS],
                young_scr[p : p + 1, lanes],
                old_scr[p : p + 1, lanes],
                reach,
            )
            state.append(jnp.where(sub == 0, 0.0, pltpu.roll(total, 1, 0)))
        direct = jnp.broadcast_to(direct_ref[0:1, lanes], (SUBS, LANES))
        for j in range(steps):
            rows = slice(j * SUBS, (j + 1) * SUBS)
            driver = work_ref[g, rows]
            if j < 2:
                driver = jnp.where(sub == 0, first_scr[j : j + 1, lanes], driver)
            keep = keep_scr[rows]
            state = [d * (keep * s) + driver for d, s in zip(decay, state)]
            local_ref[g, rows] = summed(
                [w * s for w, s in zip(weight, state)] + [direct * driver]
            )
        return carry

    lax.fori_loop(0, chans // LANES, group, 0)


def gate_kernel(
    docs_ref, halo_ref, local_ref, streams_hbm, taps_hbm,
    made_ref,
    stream_ref, taps_ref, keep_scr, alive_scr, wide_scr, sems,
):
    block_len, chans = stream_ref.shape
    steps = block_len // SUBS
    copies = [
        pltpu.make_async_copy(taps_hbm, taps_ref, sems.at[0]),
        pltpu.make_async_copy(streams_hbm.at[0], stream_ref, sems.at[1]),
    ]
    for c in copies:
        c.start()
    first = lax.axis_index("seq") * block_len
    starts = start_positions(docs_ref, docs_ref.shape[0])
    base = first + steps * lax.broadcasted_iota(jnp.int32, (SUBS, LANES), 0)
    for j in range(steps):
        rows = slice(j * SUBS, (j + 1) * SUBS)
        keep_scr[rows] = keep_rows(starts, base + j)
        alive = jnp.ones((SUBS, LANES), F32)
        for s in starts:
            alive = jnp.where((s >= first) & (base + j >= s), 0.0, alive)
        alive_scr[rows] = alive
    keep_before = keep_rows(starts, base - 1)
    for c in copies:
        c.wait()

    def group(g, carry):
        lanes = pl.ds(pl.multiple_of(g * LANES, LANES), LANES)
        for s in range(SUBS):
            wide_scr[s * PITCH : s * PITCH + steps] = stream_ref[
                s * steps : (s + 1) * steps, lanes
            ].astype(F32)
        taps = [jnp.broadcast_to(taps_ref[0, n : n + 1, lanes], (SUBS, LANES)) for n in range(3)]
        queries = filter_steps(
            lambda j: wide_scr[pl.ds(j, SUBS, stride=PITCH), :],
            halo_ref[0, :, lanes].astype(F32),
            taps,
            lambda j: keep_scr[j * SUBS : (j + 1) * SUBS],
            keep_before,
            steps,
        )
        local, asked = [], []
        for j, query in enumerate(queries):
            rows = slice(j * SUBS, (j + 1) * SUBS)
            local.append(query * local_ref[g, rows])
            asked.append(query * alive_scr[rows])
            if j % 2 == 1:
                rows = slice((j - 1) * SUBS, (j + 1) * SUBS)
                made_ref[0, rows, lanes] = jnp.concatenate(local).astype(BF16)
                made_ref[1, rows, lanes] = jnp.concatenate(asked).astype(BF16)
                local, asked = [], []
        return carry

    lax.fori_loop(0, chans // LANES, group, 0)


def summed(terms):
    while len(terms) > 1:
        paired = [a + b for a, b in zip(terms[::2], terms[1::2])]
        terms = paired + ([terms[-1]] if len(terms) % 2 else [])
    return terms[0]


def out_kernel(
    docs_ref, rates_ref, before_ref, made_ref, unembed_hbm, *totals_and_rest,
    block_len, row_members, rows_back,
):
    totals = totals_and_rest[:rows_back]
    (
        gated_hbm, logits_ref,
        unembed_ref, gated_ref, arriving_scr, out_scr, sem, gated_sems,
    ) = totals_and_rest[rows_back:]
    poles, chans = rates_ref.shape
    steps = block_len // SUBS
    groups = chans // LANES
    copy = pltpu.make_async_copy(unembed_hbm, unembed_ref, sem)
    gated_copies = []
    copy.start()
    block = lax.axis_index("seq")
    first = block * block_len
    row = lax.div(block, row_members)
    me = lax.rem(block, row_members)
    row_len = block_len * row_members
    starts = start_positions(docs_ref, docs_ref.shape[0])

    rates = rates_ref[...]
    row_transfer = jnp.exp(-rates * row_len)
    total = jnp.zeros(rates.shape, F32)
    for back in range(rows_back, 0, -1):
        low = (row - back) * row_len
        clean = no_start_in(starts, low, low + row_len)
        total = (row_transfer * clean) * total + totals[back - 1][...].astype(F32)
    within = jnp.exp(-rates * (me * block_len).astype(F32)) * no_start_in(
        starts, row * row_len, first
    )
    arriving_scr[...] = before_ref[...] + within * total
    sub = lax.broadcasted_iota(jnp.int32, (SUBS, LANES), 0)

    share = logits_ref.shape[1]
    for g in range(groups):
        lanes = slice(g * LANES, (g + 1) * LANES)
        decay, fading = [], []
        for p in range(poles):
            rate = jnp.broadcast_to(rates_ref[p : p + 1, lanes], (SUBS, LANES))
            decay.append(jnp.exp(-rate))
            fading.append(
                jnp.exp(-rate * (steps * sub).astype(F32)) * arriving_scr[p : p + 1, lanes]
            )
        for j in range(steps):
            if j % 2 == 0:
                both_rows = slice(j * SUBS, (j + 2) * SUBS)
                local = made_ref[0, both_rows, lanes].astype(F32)
                asked = made_ref[1, both_rows, lanes].astype(F32)
            half = slice((j % 2) * SUBS, (j % 2 + 1) * SUBS)
            out_scr[pl.ds(j, SUBS, stride=PITCH), :] = (
                local[half] + asked[half] * summed(fading)
            )
            fading = [d * f for d, f in zip(decay, fading)]
        for s in range(SUBS):
            gated_ref[s * steps : (s + 1) * steps, lanes] = out_scr[
                s * PITCH : s * PITCH + steps
            ].astype(BF16)
        if g % 2 == 1:
            both = slice((g - 1) * LANES, (g + 1) * LANES)
            gated_copies.append(
                pltpu.make_async_copy(
                    gated_ref.at[:, both], gated_hbm.at[:, both], gated_sems.at[g // 2]
                )
            )
            gated_copies[-1].start()
    copy.wait()
    logits = jnp.dot(gated_ref[...], unembed_ref[...], preferred_element_type=F32).astype(BF16)
    for i in range(logits_ref.shape[0]):
        logits_ref[i] = logits[i * share : (i + 1) * share]
    for c in gated_copies:
        c.wait()


def loss_kernel(targets_ref, parts_ref, loss_ref):
    members, share, vocab = parts_ref.shape
    logits = parts_ref[0].astype(F32)
    for i in range(1, members):
        logits = logits + parts_ref[i].astype(F32)
    place = lax.axis_index("chan")
    first = place * share
    row = lax.broadcasted_iota(jnp.int32, (share, 1), 0)
    target = jnp.zeros((share, 1), jnp.int32)
    for t in range(share):
        target = jnp.where(row == t, targets_ref[first + t], target)
    peak = jnp.max(logits, axis=1, keepdims=True)
    total = jnp.sum(jnp.exp(logits - peak), axis=1, keepdims=True)
    ids = lax.broadcasted_iota(jnp.int32, logits.shape, 1)
    picked = jnp.sum(jnp.where(ids == target, logits, 0.0), axis=1, keepdims=True)
    loss = peak + jnp.log(total) - picked
    lines, wide = loss_ref.shape[1:]
    lane = lax.broadcasted_iota(jnp.int32, (share, wide), 1)
    mine = lane == lax.rem(first, wide) + lax.broadcasted_iota(jnp.int32, (share, wide), 0)
    line = jnp.sum(jnp.where(mine, loss, 0.0), axis=0, keepdims=True)
    at = lax.broadcasted_iota(jnp.int32, (lines, wide), 0) == lax.div(first, wide)
    placed = jnp.where(at, line, 0.0)
    for i in range(loss_ref.shape[0]):
        loss_ref[i] = placed


def in_vmem(count):
    return [pl.BlockSpec(memory_space=pltpu.VMEM)] * count


def in_hbm(count):
    return [pl.BlockSpec(memory_space=pltpu.HBM)] * count


def kept_in_hbm(*arrays):
    return [pltpu.with_memory_space_constraint(x, pltpu.HBM) for x in arrays]


def kept_in_vmem(*arrays):
    return [pltpu.with_memory_space_constraint(x, pltpu.VMEM) for x in arrays]


def in_smem(count):
    return [pl.BlockSpec(memory_space=pltpu.SMEM)] * count


PARAMS = pltpu.CompilerParams(vmem_limit_bytes=VMEM_LIMIT)


def local(row_members, streams, short_filter, pole_rates, residues, direct, doc_lengths, targets, unembed):
    block_len, chans = streams.shape[1:]
    poles = pole_rates.shape[0]
    vocab = unembed.shape[1]
    seq, chan = lax.axis_size("seq"), lax.axis_size("chan")
    rows = seq // row_members
    share = block_len // chan
    groups = chans // LANES
    halo = lax.ppermute(
        streams[:, block_len - 2 :, :], "seq", [(i, i + 1) for i in range(seq - 1)]
    )
    work = pl.pallas_call(
        first_kernel,
        out_shape=pltpu.VMEM((groups, block_len + SUBS * (1 + poles), LANES), F32),
        in_specs=in_hbm(4),
        out_specs=in_vmem(1)[0],
        scratch_shapes=[
            pltpu.SMEM(doc_lengths.shape, jnp.int32),
            pltpu.VMEM((2, block_len, chans), BF16),
            pltpu.VMEM(short_filter.shape, F32),
            pltpu.VMEM(pole_rates.shape, F32),
            pltpu.VMEM((block_len, LANES), F32),
            pltpu.VMEM((block_len, LANES), F32),
            pltpu.VMEM((2, SUBS * PITCH, LANES), F32),
            pltpu.SemaphoreType.DMA((3,)),
            pltpu.SemaphoreType.DMA((groups,)),
        ],
        compiler_params=PARAMS,
        cost_estimate=pl.CostEstimate(
            flops=60 * block_len * chans, bytes_accessed=4 * streams.size, transcendentals=0
        ),
        name="block_states",
    )(*kept_in_hbm(doc_lengths, streams, short_filter, pole_rates))
    ends = pl.pallas_call(
        functools.partial(join_kernel, block_len=block_len),
        out_shape=pltpu.VMEM((row_members, poles, chans), BF16),
        in_specs=in_smem(1) + in_vmem(5),
        out_specs=in_vmem(1)[0],
        compiler_params=PARAMS,
        name="joined_states",
    )(doc_lengths, halo, short_filter, pole_rates, residues, *kept_in_vmem(work))
    along_row = [[r * row_members + i for i in range(row_members)] for r in range(rows)]
    ends = lax.all_to_all(ends, "seq", 0, 0, axis_index_groups=along_row)
    local_out = pl.pallas_call(
        functools.partial(local_kernel, block_len=block_len),
        out_shape=pltpu.VMEM((groups, block_len, LANES), F32),
        in_specs=in_smem(1) + in_vmem(2) + in_hbm(4),
        out_specs=in_vmem(1)[0],
        scratch_shapes=[
            pltpu.VMEM(short_filter.shape, F32),
            pltpu.VMEM(pole_rates.shape, F32),
            pltpu.VMEM(residues.shape, F32),
            pltpu.VMEM((1, chans), F32),
            pltpu.VMEM((block_len, LANES), F32),
            pltpu.VMEM((poles, chans), F32),
            pltpu.VMEM((poles, chans), F32),
            pltpu.VMEM((poles, chans), F32),
            pltpu.VMEM((2, chans), F32),
            pltpu.SemaphoreType.DMA((4,)),
        ],
        compiler_params=PARAMS,
        cost_estimate=pl.CostEstimate(
            flops=100 * block_len * chans, bytes_accessed=8 * streams.size, transcendentals=0
        ),
        name="local_out",
    )(
        doc_lengths, halo, *kept_in_vmem(work),
        *kept_in_hbm(short_filter, pole_rates, residues, direct[None]),
    )
    ends, local_out = lax.optimization_barrier((ends, local_out))
    total, before = pl.pallas_call(
        functools.partial(row_kernel, block_len=block_len),
        out_shape=(pltpu.VMEM((poles, chans), BF16), pltpu.VMEM((poles, chans), F32)),
        in_specs=in_smem(1) + in_vmem(2),
        out_specs=in_vmem(2),
        compiler_params=PARAMS,
        name="row_states",
    )(doc_lengths, pole_rates, ends)
    total, local_out, halo = lax.optimization_barrier((total, local_out, halo))
    rows_back = min(rows - 1, -(-LONGEST // (block_len * row_members)))
    totals = [
        lax.ppermute(total, "seq", [(i, i + row_members * k) for i in range(seq - row_members * k)])
        for k in range(1, rows_back + 1)
    ]
    made = pl.pallas_call(
        gate_kernel,
        out_shape=pltpu.VMEM((2, block_len, chans), BF16),
        in_specs=in_smem(1) + in_vmem(2) + in_hbm(2),
        out_specs=in_vmem(1)[0],
        scratch_shapes=[
            pltpu.VMEM((block_len, chans), BF16),
            pltpu.VMEM(short_filter.shape, F32),
            pltpu.VMEM((block_len, LANES), F32),
            pltpu.VMEM((block_len, LANES), F32),
            pltpu.VMEM((SUBS * PITCH, LANES), F32),
            pltpu.SemaphoreType.DMA((2,)),
        ],
        compiler_params=PARAMS,
        cost_estimate=pl.CostEstimate(
            flops=50 * block_len * chans, bytes_accessed=4 * streams.size, transcendentals=0
        ),
        name="gated_local",
    )(doc_lengths, halo, *kept_in_vmem(local_out), *kept_in_hbm(streams, short_filter))
    gated, logits = pl.pallas_call(
        functools.partial(
            out_kernel, block_len=block_len, row_members=row_members, rows_back=rows_back
        ),
        out_shape=(
            jax.ShapeDtypeStruct((block_len, chans), BF16),
            pltpu.VMEM((chan, share, vocab), BF16),
        ),
        in_specs=in_smem(1) + in_vmem(3) + in_hbm(1) + in_vmem(rows_back),
        out_specs=in_hbm(1) + in_vmem(1),
        scratch_shapes=[
            pltpu.VMEM(unembed.shape, BF16),
            pltpu.VMEM((block_len, chans), BF16),
            pltpu.VMEM((poles, chans), F32),
            pltpu.VMEM((SUBS * PITCH, LANES), F32),
            pltpu.SemaphoreType.DMA,
            pltpu.SemaphoreType.DMA((groups // 2,)),
        ],
        compiler_params=PARAMS,
        name="gated_logits",
    )(doc_lengths, pole_rates, *kept_in_vmem(before, made), *kept_in_hbm(unembed), *totals)
    parts = lax.all_to_all(logits, "chan", 0, 0)
    losses = pl.pallas_call(
        loss_kernel,
        out_shape=pltpu.VMEM((chan, block_len // LANES, LANES), F32),
        in_specs=in_smem(1) + in_vmem(1),
        out_specs=pl.BlockSpec(memory_space=pltpu.VMEM),
        compiler_params=PARAMS,
        name="token_losses",
    )(targets, parts)
    losses = lax.all_to_all(losses, "chan", 0, 0)
    return gated, jnp.sum(losses, axis=0).reshape(block_len)


def solution(mesh):
    seq = mesh.shape["seq"]
    row_members = 16 if seq % 16 == 0 else seq
    in_specs = (
        P(None, "seq", "chan"),
        P(None, None, "chan"),
        P(None, "chan"),
        P(None, "chan"),
        P("chan"),
        P(),
        P("seq"),
        P("chan", None),
    )
    out_specs = (P("seq", "chan"), P("seq"))
    return jax.shard_map(
        functools.partial(local, row_members),
        mesh=mesh,
        in_specs=in_specs,
        out_specs=out_specs,
        check_vma=False,
    )
```

```python
import functools

import jax
import jax.numpy as jnp
from jax import lax
from jax.experimental import pallas as pl
from jax.experimental.pallas import tpu as pltpu
from jax.sharding import PartitionSpec as P

F32 = jnp.float32
BF16 = jnp.bfloat16
LANES = 128
SUBS = 8
PITCH = 40
LONGEST = 8192
VMEM_LIMIT = 16 * 1024 * 1024


def start_positions(docs_ref, count):
    starts = [jnp.int32(0)]
    for i in range(count - 1):
        starts.append(starts[-1] + docs_ref[i])
    return starts


def no_start_in(starts, low, high):
    clean = jnp.float32(1.0)
    for s in starts:
        clean = jnp.where((s >= low) & (s < high), jnp.float32(0.0), clean)
    return clean


def keep_rows(starts, position):
    keep = jnp.ones(position.shape, F32)
    for s in starts:
        keep = jnp.where(position == s, 0.0, keep)
    return keep


def shifted_down(rows, top):
    sub = lax.broadcasted_iota(jnp.int32, rows.shape, 0)
    return jnp.where(sub == 0, top, pltpu.roll(rows, 1, 0))


def filter_steps(load, halo, taps, keep_at, keep_before, steps):
    last = load(steps - 1)
    previous = shifted_down(last, halo[1:2])
    masked_before = keep_before * shifted_down(load(steps - 2), halo[0:1])
    for j in range(steps):
        now = load(j)
        keep = keep_at(j)
        masked = keep * previous
        yield taps[0] * now + taps[1] * masked + taps[2] * (keep * masked_before)
        masked_before = masked
        previous = now


def first_kernel(
    docs_hbm, streams_hbm, taps_hbm, rates_hbm,
    work_ref,
    docs_ref, streams_ref, taps_ref, rates_ref, keep_scr, tail_scr, wide_scr, sems, group_sems,
):
    poles, chans = rates_ref.shape
    block_len = streams_ref.shape[1]
    steps = block_len // SUBS
    groups = chans // LANES
    copies = [
        pltpu.make_async_copy(docs_hbm, docs_ref, sems.at[0]),
        pltpu.make_async_copy(taps_hbm, taps_ref, sems.at[1]),
        pltpu.make_async_copy(rates_hbm, rates_ref, sems.at[2]),
    ]

    def group_copy(g):
        lanes = pl.ds(pl.multiple_of(g * LANES, LANES), LANES)
        return pltpu.make_async_copy(
            streams_hbm.at[1:3, :, lanes], streams_ref.at[:, :, lanes], group_sems.at[g]
        )

    for c in copies:
        c.start()
    for g in range(groups):
        group_copy(g).start()
    first = lax.axis_index("seq") * block_len
    for c in copies:
        c.wait()
    starts = start_positions(docs_ref, docs_ref.shape[0])
    base = first + steps * lax.broadcasted_iota(jnp.int32, (SUBS, LANES), 0)
    keep_before = keep_rows(starts, base - 1)
    tail = jnp.ones((SUBS, LANES), F32)
    for j in reversed(range(steps)):
        keep = keep_rows(starts, base + j)
        keep_scr[j * SUBS : (j + 1) * SUBS] = keep
        tail_scr[j * SUBS : (j + 1) * SUBS] = tail
        tail = tail * keep
    nothing = jnp.zeros((2, LANES), F32)

    def group(g, carry):
        group_copy(g).wait()
        lanes = pl.ds(pl.multiple_of(g * LANES, LANES), LANES)
        for i in range(2):
            for s in range(SUBS):
                wide_scr[i, s * PITCH : s * PITCH + steps] = streams_ref[
                    i, s * steps : (s + 1) * steps, lanes
                ].astype(F32)

        def steps_of(i):
            taps = [
                jnp.broadcast_to(taps_ref[i + 1, n : n + 1, lanes], (SUBS, LANES))
                for n in range(3)
            ]
            return filter_steps(
                lambda j: wide_scr[i, pl.ds(j, SUBS, stride=PITCH), :],
                nothing,
                taps,
                lambda j: keep_scr[j * SUBS : (j + 1) * SUBS],
                keep_before,
                steps,
            )

        decays = jnp.exp(-rates_ref[:, lanes])
        decay = [jnp.broadcast_to(decays[p : p + 1], (SUBS, LANES)) for p in range(poles)]
        state = [jnp.zeros((SUBS, LANES), F32) for _ in range(poles)]
        for j, (key, value) in enumerate(zip(steps_of(0), steps_of(1))):
            rows = slice(j * SUBS, (j + 1) * SUBS)
            if j < 2:
                work_ref[g, block_len + j : block_len + 1 + j] = key[0:1]
                work_ref[g, block_len + 2 + j : block_len + 3 + j] = value[0:1]
            driver = key * value
            work_ref[g, rows] = driver
            masked = driver * tail_scr[rows]
            state = [d * s + masked for d, s in zip(decay, state)]
        for p in range(poles):
            at = block_len + SUBS * (1 + p)
            work_ref[g, at : at + SUBS] = state[p]
        return carry

    lax.fori_loop(0, groups, group, 0)


def edge_marks(starts, first, steps):
    older = no_start_in(starts, first - 1, first)
    keep = [no_start_in(starts, first + j, first + j + 1) for j in range(2)]
    counts = [no_start_in(starts, first + j + 1, first + steps) for j in range(2)]
    return older, keep, counts


def corrected(marks, halo_ref, taps_ref, edge, lanes):
    older, keep, counts = marks

    def added(i):
        halo = halo_ref[i, :, lanes].astype(F32)
        taps = taps_ref[i, :, lanes]
        near = (keep[0] * taps[1:2]) * halo[1:2] + (keep[0] * older * taps[2:3]) * halo[0:1]
        return near, (keep[1] * keep[0] * taps[2:3]) * halo[1:2]

    key, value = added(1), added(2)
    drivers, changes = [], []
    for j in range(2):
        old_key, old_value = edge[j : j + 1], edge[2 + j : 3 + j]
        driver = (old_key + key[j]) * (old_value + value[j])
        drivers.append(driver)
        changes.append(counts[j] * (driver - old_key * old_value))
    return drivers, changes


def chunk_reach(starts, first, steps):
    sub = lax.broadcasted_iota(jnp.int32, (SUBS, LANES), 0)
    base = first + steps * sub
    clean = jnp.ones((SUBS, LANES), F32)
    for s in starts:
        clean = jnp.where((s >= base) & (s < base + steps), 0.0, clean)
    reach = [clean]
    for k in (1, 2):
        reach.append(reach[-1] * jnp.where(sub >= k, pltpu.roll(reach[-1], k, 0), 0.0))
    return [jnp.where(sub >= k, r, 0.0) for k, r in zip((1, 2, 4), reach)]


def chunk_ends(state, young, power, reach):
    sub = lax.broadcasted_iota(jnp.int32, (SUBS, LANES), 0)
    total = state + jnp.where(sub == 0, young, 0.0)
    power = jnp.broadcast_to(power, (SUBS, LANES))
    for k, r in zip((1, 2, 4), reach):
        total = total + (power * r) * pltpu.roll(total, k, 0)
        power = power * power
    return total


def join_kernel(
    docs_ref, halo_ref, taps_ref, rates_ref, residues_ref, work_ref, ends_ref, *, block_len
):
    poles, chans = rates_ref.shape
    steps = block_len // SUBS
    first = lax.axis_index("seq") * block_len
    starts = start_positions(docs_ref, docs_ref.shape[0])
    marks = edge_marks(starts, first, steps)
    clean = [
        no_start_in(starts, first + s * steps, first + (s + 1) * steps) for s in range(SUBS)
    ]
    for g in range(chans // LANES):
        lanes = slice(g * LANES, (g + 1) * LANES)
        edge = work_ref[g, block_len : block_len + SUBS]
        _, changes = corrected(marks, halo_ref, taps_ref, edge, lanes)
        rates = rates_ref[:, lanes]
        decays = jnp.exp(-rates)
        transfer = jnp.exp(-rates * steps)
        total = jnp.exp(-rates * (steps - 2)) * (decays * changes[0] + changes[1])
        for s in range(SUBS):
            if s > 0:
                total = (transfer * clean[s]) * total
            total = total + work_ref[g, pl.ds(block_len + SUBS + s, poles, stride=SUBS), :]
        ends = (residues_ref[:, lanes] * ((1.0 - decays) * decays) * total).astype(BF16)
        for i in range(ends_ref.shape[0]):
            ends_ref[i, :, lanes] = ends


def row_kernel(docs_ref, rates_ref, ends_ref, total_ref, before_ref, *, block_len):
    members = ends_ref.shape[0]
    block = lax.axis_index("seq")
    first = block * block_len
    me = lax.rem(block, members)
    row_first = first - me * block_len
    starts = start_positions(docs_ref, docs_ref.shape[0])
    transfer = jnp.exp(-rates_ref[...] * block_len)
    total = jnp.zeros(transfer.shape, F32)
    before = jnp.zeros(transfer.shape, F32)
    for j in range(members):
        before = jnp.where(me == j, total, before)
        low = row_first + j * block_len
        total = (transfer * no_start_in(starts, low, low + block_len)) * total + ends_ref[j].astype(F32)
    total_ref[...] = total.astype(BF16)
    before_ref[...] = before


def local_kernel(
    docs_ref, halo_ref, work_ref, taps_hbm, rates_hbm, residues_hbm, direct_hbm,
    local_ref,
    taps_ref, rates_ref, residues_ref, direct_ref,
    keep_scr, weight_scr, old_scr, young_scr, first_scr, sems,
    *, block_len,
):
    poles, chans = rates_ref.shape
    steps = block_len // SUBS
    copies = [
        pltpu.make_async_copy(source, target, sems.at[i])
        for i, (source, target) in enumerate(
            (
                (taps_hbm, taps_ref),
                (rates_hbm, rates_ref),
                (residues_hbm, residues_ref),
                (direct_hbm, direct_ref),
            )
        )
    ]
    for c in copies:
        c.start()
    first = lax.axis_index("seq") * block_len
    starts = start_positions(docs_ref, docs_ref.shape[0])
    sub = lax.broadcasted_iota(jnp.int32, (SUBS, LANES), 0)
    base = first + steps * sub
    for j in range(steps):
        keep_scr[j * SUBS : (j + 1) * SUBS] = keep_rows(starts, base + j)
    reach = chunk_reach(starts, first, steps)
    for c in copies:
        c.wait()
    rates = rates_ref[...]
    decays = jnp.exp(-rates)
    weight_scr[...] = residues_ref[...] * (1.0 - decays)
    older = jnp.exp(-rates * (steps - 2))
    old_scr[...] = jnp.exp(-rates * steps)
    marks = edge_marks(starts, first, steps)
    for g in range(chans // LANES):
        lanes = slice(g * LANES, (g + 1) * LANES)
        edge = work_ref[g, block_len : block_len + SUBS]
        drivers, changes = corrected(marks, halo_ref, taps_ref, edge, lanes)
        young_scr[:, lanes] = older[:, lanes] * (decays[:, lanes] * changes[0] + changes[1])
        for j in range(2):
            first_scr[j : j + 1, lanes] = drivers[j]

    def group(g, carry):
        lanes = pl.ds(pl.multiple_of(g * LANES, LANES), LANES)
        decays = jnp.exp(-rates_ref[:, lanes])
        decay, weight, state = [], [], []
        for p in range(poles):
            decay.append(jnp.broadcast_to(decays[p : p + 1], (SUBS, LANES)))
            weight.append(jnp.broadcast_to(weight_scr[p : p + 1, lanes], (SUBS, LANES)))
            at = block_len + SUBS * (1 + p)
            total = chunk_ends(
                work_ref[g, at : at + SUBS],
                young_scr[p : p + 1, lanes],
                old_scr[p : p + 1, lanes],
                reach,
            )
            state.append(jnp.where(sub == 0, 0.0, pltpu.roll(total, 1, 0)))
        direct = jnp.broadcast_to(direct_ref[0:1, lanes], (SUBS, LANES))
        for j in range(steps):
            rows = slice(j * SUBS, (j + 1) * SUBS)
            driver = work_ref[g, rows]
            if j < 2:
                driver = jnp.where(sub == 0, first_scr[j : j + 1, lanes], driver)
            keep = keep_scr[rows]
            state = [d * (keep * s) + driver for d, s in zip(decay, state)]
            local_ref[g, rows] = summed(
                [w * s for w, s in zip(weight, state)] + [direct * driver]
            )
        return carry

    lax.fori_loop(0, chans // LANES, group, 0)


def gate_kernel(
    docs_ref, halo_ref, local_ref, streams_hbm, taps_hbm,
    made_ref,
    stream_ref, taps_ref, keep_scr, alive_scr, wide_scr, sems,
):
    block_len, chans = stream_ref.shape
    steps = block_len // SUBS
    copies = [
        pltpu.make_async_copy(taps_hbm, taps_ref, sems.at[0]),
        pltpu.make_async_copy(streams_hbm.at[0], stream_ref, sems.at[1]),
    ]
    for c in copies:
        c.start()
    first = lax.axis_index("seq") * block_len
    starts = start_positions(docs_ref, docs_ref.shape[0])
    base = first + steps * lax.broadcasted_iota(jnp.int32, (SUBS, LANES), 0)
    for j in range(steps):
        rows = slice(j * SUBS, (j + 1) * SUBS)
        keep_scr[rows] = keep_rows(starts, base + j)
        alive = jnp.ones((SUBS, LANES), F32)
        for s in starts:
            alive = jnp.where((s >= first) & (base + j >= s), 0.0, alive)
        alive_scr[rows] = alive
    keep_before = keep_rows(starts, base - 1)
    for c in copies:
        c.wait()

    def group(g, carry):
        lanes = pl.ds(pl.multiple_of(g * LANES, LANES), LANES)
        for s in range(SUBS):
            wide_scr[s * PITCH : s * PITCH + steps] = stream_ref[
                s * steps : (s + 1) * steps, lanes
            ].astype(F32)
        taps = [jnp.broadcast_to(taps_ref[0, n : n + 1, lanes], (SUBS, LANES)) for n in range(3)]
        queries = filter_steps(
            lambda j: wide_scr[pl.ds(j, SUBS, stride=PITCH), :],
            halo_ref[0, :, lanes].astype(F32),
            taps,
            lambda j: keep_scr[j * SUBS : (j + 1) * SUBS],
            keep_before,
            steps,
        )
        local, asked = [], []
        for j, query in enumerate(queries):
            rows = slice(j * SUBS, (j + 1) * SUBS)
            local.append(query * local_ref[g, rows])
            asked.append(query * alive_scr[rows])
            if j % 2 == 1:
                rows = slice((j - 1) * SUBS, (j + 1) * SUBS)
                made_ref[0, rows, lanes] = jnp.concatenate(local).astype(BF16)
                made_ref[1, rows, lanes] = jnp.concatenate(asked).astype(BF16)
                local, asked = [], []
        return carry

    lax.fori_loop(0, chans // LANES, group, 0)


def summed(terms):
    while len(terms) > 1:
        paired = [a + b for a, b in zip(terms[::2], terms[1::2])]
        terms = paired + ([terms[-1]] if len(terms) % 2 else [])
    return terms[0]


def out_kernel(
    docs_ref, rates_ref, before_ref, made_ref, unembed_hbm, *totals_and_rest,
    block_len, row_members, rows_back,
):
    totals = totals_and_rest[:rows_back]
    (
        gated_hbm, logits_ref,
        unembed_ref, gated_ref, arriving_scr, out_scr, sem, gated_sems,
    ) = totals_and_rest[rows_back:]
    poles, chans = rates_ref.shape
    steps = block_len // SUBS
    groups = chans // LANES
    copy = pltpu.make_async_copy(unembed_hbm, unembed_ref, sem)
    gated_copies = []
    copy.start()
    block = lax.axis_index("seq")
    first = block * block_len
    row = lax.div(block, row_members)
    me = lax.rem(block, row_members)
    row_len = block_len * row_members
    starts = start_positions(docs_ref, docs_ref.shape[0])

    rates = rates_ref[...]
    row_transfer = jnp.exp(-rates * row_len)
    total = jnp.zeros(rates.shape, F32)
    for back in range(rows_back, 0, -1):
        low = (row - back) * row_len
        clean = no_start_in(starts, low, low + row_len)
        total = (row_transfer * clean) * total + totals[back - 1][...].astype(F32)
    within = jnp.exp(-rates * (me * block_len).astype(F32)) * no_start_in(
        starts, row * row_len, first
    )
    arriving_scr[...] = before_ref[...] + within * total
    sub = lax.broadcasted_iota(jnp.int32, (SUBS, LANES), 0)

    share = logits_ref.shape[1]
    for g in range(groups):
        lanes = slice(g * LANES, (g + 1) * LANES)
        decay, fading = [], []
        for p in range(poles):
            rate = jnp.broadcast_to(rates_ref[p : p + 1, lanes], (SUBS, LANES))
            decay.append(jnp.exp(-rate))
            fading.append(
                jnp.exp(-rate * (steps * sub).astype(F32)) * arriving_scr[p : p + 1, lanes]
            )
        for j in range(steps):
            if j % 2 == 0:
                both_rows = slice(j * SUBS, (j + 2) * SUBS)
                local = made_ref[0, both_rows, lanes].astype(F32)
                asked = made_ref[1, both_rows, lanes].astype(F32)
            half = slice((j % 2) * SUBS, (j % 2 + 1) * SUBS)
            out_scr[pl.ds(j, SUBS, stride=PITCH), :] = (
                local[half] + asked[half] * summed(fading)
            )
            fading = [d * f for d, f in zip(decay, fading)]
        for s in range(SUBS):
            gated_ref[s * steps : (s + 1) * steps, lanes] = out_scr[
                s * PITCH : s * PITCH + steps
            ].astype(BF16)
        if g % 2 == 1:
            both = slice((g - 1) * LANES, (g + 1) * LANES)
            gated_copies.append(
                pltpu.make_async_copy(
                    gated_ref.at[:, both], gated_hbm.at[:, both], gated_sems.at[g // 2]
                )
            )
            gated_copies[-1].start()
    copy.wait()
    logits = jnp.dot(gated_ref[...], unembed_ref[...], preferred_element_type=F32).astype(BF16)
    for i in range(logits_ref.shape[0]):
        logits_ref[i] = logits[i * share : (i + 1) * share]
    for c in gated_copies:
        c.wait()


def loss_kernel(targets_ref, parts_ref, loss_ref):
    members, share, vocab = parts_ref.shape
    logits = parts_ref[0].astype(F32)
    for i in range(1, members):
        logits = logits + parts_ref[i].astype(F32)
    place = lax.axis_index("chan")
    first = place * share
    lines, wide = loss_ref.shape[1:]
    lane = lax.broadcasted_iota(jnp.int32, (share, wide), 1)
    mine = lane == lax.rem(first, wide) + lax.broadcasted_iota(jnp.int32, (share, wide), 0)
    near = targets_ref[pl.ds(lax.div(first, wide), 1), :].astype(F32)
    target = jnp.sum(jnp.where(mine, near, 0.0), axis=1, keepdims=True).astype(jnp.int32)
    peak = jnp.max(logits, axis=1, keepdims=True)
    total = jnp.sum(jnp.exp(logits - peak), axis=1, keepdims=True)
    ids = lax.broadcasted_iota(jnp.int32, logits.shape, 1)
    picked = jnp.sum(jnp.where(ids == target, logits, 0.0), axis=1, keepdims=True)
    loss = peak + jnp.log(total) - picked
    line = jnp.sum(jnp.where(mine, loss, 0.0), axis=0, keepdims=True)
    at = lax.broadcasted_iota(jnp.int32, (lines, wide), 0) == lax.div(first, wide)
    placed = jnp.where(at, line, 0.0)
    for i in range(loss_ref.shape[0]):
        loss_ref[i] = placed


def in_vmem(count):
    return [pl.BlockSpec(memory_space=pltpu.VMEM)] * count


def in_hbm(count):
    return [pl.BlockSpec(memory_space=pltpu.HBM)] * count


def kept_in_hbm(*arrays):
    return [pltpu.with_memory_space_constraint(x, pltpu.HBM) for x in arrays]


def kept_in_vmem(*arrays):
    return [pltpu.with_memory_space_constraint(x, pltpu.VMEM) for x in arrays]


def in_smem(count):
    return [pl.BlockSpec(memory_space=pltpu.SMEM)] * count


PARAMS = pltpu.CompilerParams(vmem_limit_bytes=VMEM_LIMIT)


def local(row_members, streams, short_filter, pole_rates, residues, direct, doc_lengths, targets, unembed):
    block_len, chans = streams.shape[1:]
    poles = pole_rates.shape[0]
    vocab = unembed.shape[1]
    seq, chan = lax.axis_size("seq"), lax.axis_size("chan")
    rows = seq // row_members
    share = block_len // chan
    groups = chans // LANES
    halo = lax.ppermute(
        streams[:, block_len - 2 :, :], "seq", [(i, i + 1) for i in range(seq - 1)]
    )
    work = pl.pallas_call(
        first_kernel,
        out_shape=pltpu.VMEM((groups, block_len + SUBS * (1 + poles), LANES), F32),
        in_specs=in_hbm(4),
        out_specs=in_vmem(1)[0],
        scratch_shapes=[
            pltpu.SMEM(doc_lengths.shape, jnp.int32),
            pltpu.VMEM((2, block_len, chans), BF16),
            pltpu.VMEM(short_filter.shape, F32),
            pltpu.VMEM(pole_rates.shape, F32),
            pltpu.VMEM((block_len, LANES), F32),
            pltpu.VMEM((block_len, LANES), F32),
            pltpu.VMEM((2, SUBS * PITCH, LANES), F32),
            pltpu.SemaphoreType.DMA((3,)),
            pltpu.SemaphoreType.DMA((groups,)),
        ],
        compiler_params=PARAMS,
        cost_estimate=pl.CostEstimate(
            flops=60 * block_len * chans, bytes_accessed=4 * streams.size, transcendentals=0
        ),
        name="block_states",
    )(*kept_in_hbm(doc_lengths, streams, short_filter, pole_rates))
    ends = pl.pallas_call(
        functools.partial(join_kernel, block_len=block_len),
        out_shape=pltpu.VMEM((row_members, poles, chans), BF16),
        in_specs=in_smem(1) + in_vmem(5),
        out_specs=in_vmem(1)[0],
        compiler_params=PARAMS,
        name="joined_states",
    )(doc_lengths, halo, short_filter, pole_rates, residues, *kept_in_vmem(work))
    along_row = [[r * row_members + i for i in range(row_members)] for r in range(rows)]
    ends = lax.all_to_all(ends, "seq", 0, 0, axis_index_groups=along_row)
    local_out = pl.pallas_call(
        functools.partial(local_kernel, block_len=block_len),
        out_shape=pltpu.VMEM((groups, block_len, LANES), F32),
        in_specs=in_smem(1) + in_vmem(2) + in_hbm(4),
        out_specs=in_vmem(1)[0],
        scratch_shapes=[
            pltpu.VMEM(short_filter.shape, F32),
            pltpu.VMEM(pole_rates.shape, F32),
            pltpu.VMEM(residues.shape, F32),
            pltpu.VMEM((1, chans), F32),
            pltpu.VMEM((block_len, LANES), F32),
            pltpu.VMEM((poles, chans), F32),
            pltpu.VMEM((poles, chans), F32),
            pltpu.VMEM((poles, chans), F32),
            pltpu.VMEM((2, chans), F32),
            pltpu.SemaphoreType.DMA((4,)),
        ],
        compiler_params=PARAMS,
        cost_estimate=pl.CostEstimate(
            flops=100 * block_len * chans, bytes_accessed=8 * streams.size, transcendentals=0
        ),
        name="local_out",
    )(
        doc_lengths, halo, *kept_in_vmem(work),
        *kept_in_hbm(short_filter, pole_rates, residues, direct[None]),
    )
    ends, local_out = lax.optimization_barrier((ends, local_out))
    total, before = pl.pallas_call(
        functools.partial(row_kernel, block_len=block_len),
        out_shape=(pltpu.VMEM((poles, chans), BF16), pltpu.VMEM((poles, chans), F32)),
        in_specs=in_smem(1) + in_vmem(2),
        out_specs=in_vmem(2),
        compiler_params=PARAMS,
        name="row_states",
    )(doc_lengths, pole_rates, ends)
    total, local_out, halo = lax.optimization_barrier((total, local_out, halo))
    rows_back = min(rows - 1, -(-LONGEST // (block_len * row_members)))
    totals = [
        lax.ppermute(total, "seq", [(i, i + row_members * k) for i in range(seq - row_members * k)])
        for k in range(1, rows_back + 1)
    ]
    made = pl.pallas_call(
        gate_kernel,
        out_shape=pltpu.VMEM((2, block_len, chans), BF16),
        in_specs=in_smem(1) + in_vmem(2) + in_hbm(2),
        out_specs=in_vmem(1)[0],
        scratch_shapes=[
            pltpu.VMEM((block_len, chans), BF16),
            pltpu.VMEM(short_filter.shape, F32),
            pltpu.VMEM((block_len, LANES), F32),
            pltpu.VMEM((block_len, LANES), F32),
            pltpu.VMEM((SUBS * PITCH, LANES), F32),
            pltpu.SemaphoreType.DMA((2,)),
        ],
        compiler_params=PARAMS,
        cost_estimate=pl.CostEstimate(
            flops=50 * block_len * chans, bytes_accessed=4 * streams.size, transcendentals=0
        ),
        name="gated_local",
    )(doc_lengths, halo, *kept_in_vmem(local_out), *kept_in_hbm(streams, short_filter))
    gated, logits = pl.pallas_call(
        functools.partial(
            out_kernel, block_len=block_len, row_members=row_members, rows_back=rows_back
        ),
        out_shape=(
            jax.ShapeDtypeStruct((block_len, chans), BF16),
            pltpu.VMEM((chan, share, vocab), BF16),
        ),
        in_specs=in_smem(1) + in_vmem(3) + in_hbm(1) + in_vmem(rows_back),
        out_specs=in_hbm(1) + in_vmem(1),
        scratch_shapes=[
            pltpu.VMEM(unembed.shape, BF16),
            pltpu.VMEM((block_len, chans), BF16),
            pltpu.VMEM((poles, chans), F32),
            pltpu.VMEM((SUBS * PITCH, LANES), F32),
            pltpu.SemaphoreType.DMA,
            pltpu.SemaphoreType.DMA((groups // 2,)),
        ],
        compiler_params=PARAMS,
        name="gated_logits",
    )(doc_lengths, pole_rates, *kept_in_vmem(before, made), *kept_in_hbm(unembed), *totals)
    parts = lax.all_to_all(logits, "chan", 0, 0)
    losses = pl.pallas_call(
        loss_kernel,
        out_shape=pltpu.VMEM((chan, block_len // LANES, LANES), F32),
        in_specs=in_vmem(2),
        out_specs=pl.BlockSpec(memory_space=pltpu.VMEM),
        compiler_params=PARAMS,
        name="token_losses",
    )(targets.reshape(block_len // LANES, LANES), parts)
    losses = lax.all_to_all(losses, "chan", 0, 0)
    return gated, jnp.sum(losses, axis=0).reshape(block_len)


def solution(mesh):
    seq = mesh.shape["seq"]
    row_members = 16 if seq % 16 == 0 else seq
    in_specs = (
        P(None, "seq", "chan"),
        P(None, None, "chan"),
        P(None, "chan"),
        P(None, "chan"),
        P("chan"),
        P(),
        P("seq"),
        P("chan", None),
    )
    out_specs = (P("seq", "chan"), P("seq"))
    return jax.shard_map(
        functools.partial(local, row_members),
        mesh=mesh,
        in_specs=in_specs,
        out_specs=out_specs,
        check_vma=False,
    )
```
